768 devices in a mesh: row: 96 (over x, z, core), col: 8 (over y).
Axes of the slice: x: 4, y: 8, z: 12, core: 2. Of those that a mesh axis runs over, the one named last changes fastest.
Arguments:
- nodes: bfloat16 [196608, 128], P(('row', 'col')), may hold values from -6 to 6
- edge_feats: bfloat16 [786432, 128], P(('row', 'col')), may hold values from -6 to 6
- edge_blocks: int32 [786432, 2], P(('row', 'col')), may hold values from 0 to 19, as said below
- edge_nodes: int32 [786432, 2], P(('row', 'col')), may hold values from 0 to 127
- send_blocks: int32 [768, 8, 2], P(('row', 'col')), may hold values from 0 to 1
- send_counts: int32 [768, 8], P(('row', 'col')), may hold values from 1 to 2, as said below
- edge_w1: bfloat16 [384, 128], replicated, may hold values from -0.3125 to 0.3125
- edge_b1: float32 [128], replicated, may hold values from -3 to 3
- edge_w2: bfloat16 [128, 128], replicated, may hold values from -0.5 to 0.5
- edge_gain: float32 [128], replicated, may hold values from 0.25 to 1.75
- node_w1: bfloat16 [256, 128], replicated, may hold values from -0.375 to 0.375
- node_b1: float32 [128], replicated, may hold values from -3 to 3
- node_w2: bfloat16 [128, 128], replicated, may hold values from -0.5 to 0.5
- node_gain: float32 [128], replicated, may hold values from 0.25 to 1.75
- node_cot: bfloat16 [196608, 128], P(('row', 'col')), may hold values from -6 to 6
- edge_cot: bfloat16 [786432, 128], P(('row', 'col')), may hold values from -6 to 6
Outputs:
- node_new: bfloat16 [196608, 128], P(('row', 'col'))
- edge_new: bfloat16 [786432, 128], P(('row', 'col'))
- node_grad: float32 [196608, 128], P(('row', 'col'))
- edge_grad: bfloat16 [786432, 128], P(('row', 'col'))
- edge_w1_grad: float32 [384, 128], replicated
- edge_w2_grad: float32 [128, 128], replicated
- node_w1_grad: float32 [256, 128], replicated
- node_w2_grad: float32 [128, 128], replicated
The draws below stay inside these ranges and needn't reach their ends.
Inputs may be any that keep to these rules, and one draw needn't show every extreme that they name: `send_counts`: every device sends at least one live slot to each device of its group; some device has all 2 slots live toward every device of its group. `edge_blocks`: values below 4 name rim and own blocks; higher ones name live received slots only. Devices at the first and last row index use no missing rim block. The second column is below 2.
All inputs are finite; a program needn't handle non-finite values.
Results may differ from the reference program's by a relative error of at most 0.018.
Values may be sent and summed in bfloat16 or wider, within the bound.
No kernel may reach another device: no remote copies, remote signals or barrier semaphores. Data moves between devices by JAX's collectives and lax.ppermute only.
A program may use at most 32 MiB of HBM per device.

```python
import jax
import jax.numpy as jnp
from jax import lax

WIDTH = 128
BLOCK = 128
NBLK = 2
SLOTS = 2
BND = 1
E_DEV = 1024
NODES = 196608
EDGES = 786432
N_ROW = 96
N_COL = 8
DEVICES = 768


def counts_table(key):
    key = jax.random.fold_in(key, 11)
    devices = N_ROW * N_COL
    first, second, third = jax.random.split(key, 3)
    base = jax.random.randint(first, (devices, N_COL), 1, SLOTS + 1)
    heavy = jax.random.randint(second, (devices, 1), 0, 4) == 0
    table = jnp.where(heavy, SLOTS, base)
    spot = jax.random.randint(third, (), 0, devices)
    table = table.at[spot, :].set(SLOTS)
    return table.astype(jnp.int32)


def draw_send_counts(key, part):
    return counts_table(key)


def draw_edge_blocks(key, part):
    table = counts_table(key)
    key = jax.random.fold_in(key, 23)
    devices = N_ROW * N_COL
    total = devices * E_DEV
    kinds_key, local_key, rim_key, peer_key, slot_key, target_key = jax.random.split(key, 6)
    owner = jnp.arange(total, dtype=jnp.int32) // E_DEV
    row_of = owner // N_COL
    col_of = owner % N_COL
    kind = jax.random.randint(kinds_key, (total,), 0, 20)
    local_block = jax.random.randint(local_key, (total,), 0, NBLK) + BND
    rim_pick = jax.random.randint(rim_key, (total,), 0, 2 * BND)
    rim_block = jnp.where(rim_pick < BND, rim_pick, rim_pick + NBLK)
    rim_ok = jnp.where(rim_pick < BND, row_of > 0, row_of < N_ROW - 1)
    peer = jax.random.randint(peer_key, (total,), 0, N_COL)
    live = table[row_of * N_COL + peer, col_of]
    slot = jax.random.randint(slot_key, (total,), 0, 1 << 20) % live
    slot_block = NBLK + 2 * BND + peer * SLOTS + slot
    source = jnp.where(kind < 12, local_block, jnp.where(kind < 15, jnp.where(rim_ok, rim_block, local_block), slot_block))
    target = jax.random.randint(target_key, (total,), 0, NBLK)
    return jnp.stack([source, target], axis=1).astype(jnp.int32)


def plant(entries, own_key, least, top_value):
    spot = [jax.random.randint(jax.random.fold_in(own_key, axis), (), 0, length) for axis, length in enumerate(entries.shape)]
    longest = entries.shape.index(max(entries.shape))
    neighbour = spot[:longest] + [(spot[longest] + 1) % entries.shape[longest]] + spot[longest + 1:]
    return entries.at[tuple(spot)].set(least).at[tuple(neighbour)].set(top_value)


def level_of(key, extent, cuts, least, largest):
    factor_of = 1.0
    for axis_at, blocks in cuts:
        draws = jax.random.uniform(jax.random.fold_in(jax.random.fold_in(key, 6), axis_at), (blocks,), jnp.float32, least / len(cuts), largest / len(cuts))
        factor_of = factor_of * jnp.repeat(jnp.exp(draws), extent[axis_at] // blocks).reshape((-1,) + (1,) * (len(extent) - 1 - axis_at))
    return factor_of


def noise(key, shape, deviation, most, shards=(), kind=jnp.bfloat16):
    factor_of = level_of(key, shape, shards, -0.22, 0.18) if shards else 1.0
    values = jax.random.normal(key, shape, jnp.float32) * deviation * factor_of
    return jnp.minimum(jnp.maximum(values, -most), most).astype(kind)


def setup_inputs(seed: int = 0) -> dict:
    keys = jax.random.split(jax.random.key(seed), 17)
    return {
        "nodes": noise(keys[0], (NODES, WIDTH), 1.0, 6.0, ((0, 768),)),
        "edge_feats": noise(keys[1], (EDGES, WIDTH), 1.0, 6.0, ((0, 768),)),
        "edge_blocks": draw_edge_blocks(jax.random.fold_in(keys[16], 71), 0),
        "edge_nodes": plant(jax.random.randint(keys[3], (EDGES, 2), 0, BLOCK), jax.random.fold_in(keys[3], 1), 0, BLOCK - 1).astype(jnp.int32),
        "send_blocks": plant(jax.random.randint(keys[4], (DEVICES, N_COL, SLOTS), 0, NBLK), jax.random.fold_in(keys[4], 1), 0, NBLK - 1).astype(jnp.int32),
        "send_counts": draw_send_counts(jax.random.fold_in(keys[16], 71), 0),
        "edge_w1": noise(keys[6], (3 * WIDTH, WIDTH), (3 * WIDTH) ** -0.5, 0.3125),
        "edge_b1": noise(keys[7], (WIDTH,), 0.5, 3.0, (), jnp.float32),
        "edge_w2": noise(keys[8], (WIDTH, WIDTH), WIDTH ** -0.5, 0.5),
        "edge_gain": jnp.clip(1.0 + 0.15 * jax.random.normal(keys[9], (WIDTH,), jnp.float32), 0.25, 1.75),
        "node_w1": noise(keys[10], (2 * WIDTH, WIDTH), (2 * WIDTH) ** -0.5, 0.375),
        "node_b1": noise(keys[11], (WIDTH,), 0.5, 3.0, (), jnp.float32),
        "node_w2": noise(keys[12], (WIDTH, WIDTH), WIDTH ** -0.5, 0.5),
        "node_gain": jnp.clip(1.0 + 0.15 * jax.random.normal(keys[13], (WIDTH,), jnp.float32), 0.25, 1.75),
        "node_cot": noise(keys[14], (NODES, WIDTH), 1.0, 6.0, ((0, 768),)),
        "edge_cot": noise(keys[15], (EDGES, WIDTH), 1.0, 6.0, ((0, 768),)),
    }


EPS = 1e-05

def norm_rows(value, gain):
    mean = lax.optimization_barrier(jnp.mean(value, axis=-1, keepdims=True))
    centred = value - mean
    spread = lax.optimization_barrier(jnp.mean(centred * centred, axis=-1, keepdims=True))
    scale = lax.rsqrt(spread + EPS)
    unit = centred * scale
    return (unit * gain, unit, scale)

def norm_back(upstream, unit, scale, gain):
    along = upstream * gain
    return scale * (along - lax.optimization_barrier(jnp.mean(along, axis=-1, keepdims=True)) - unit * lax.optimization_barrier(jnp.mean(along * unit, axis=-1, keepdims=True)))

def silu_slope(first):
    sig = jax.nn.sigmoid(first)
    return sig * (1.0 + first * (1.0 - sig))

def mlp_forward(joined, w_first, b_first, w_second, gain):
    first = jnp.dot(joined, w_first, preferred_element_type=jnp.float32) + b_first
    active = jax.nn.silu(first).astype(jnp.bfloat16)
    second = jnp.dot(active, w_second, preferred_element_type=jnp.float32)
    out, unit, scale = norm_rows(second, gain)
    return (out, (first, active, unit, scale))

def mlp_backward(upstream, joined, saved, w_first, w_second, gain):
    first, active, unit, scale = saved
    d_second = norm_back(upstream, unit, scale, gain).astype(jnp.bfloat16)
    g_second = jnp.dot(active.T, d_second, preferred_element_type=jnp.float32)
    d_active = jnp.dot(d_second, w_second.T, preferred_element_type=jnp.float32)
    d_first = (d_active * silu_slope(first)).astype(jnp.bfloat16)
    g_first = jnp.dot(joined.T, d_first, preferred_element_type=jnp.float32)
    d_joined = jnp.dot(d_first, w_first.T, preferred_element_type=jnp.float32)
    return (d_joined, g_first, g_second)

def source_rows(edge_blocks, edge_nodes, send_blocks, send_counts):
    devices = N_ROW * N_COL
    owner = jnp.arange(devices * E_DEV, dtype=jnp.int32) // E_DEV
    row_of = owner // N_COL
    col_of = owner % N_COL
    block = edge_blocks[:, 0]
    base = NBLK + 2 * BND
    peer = jnp.clip((block - base) // SLOTS, 0, N_COL - 1)
    slot = jnp.clip(block - base - peer * SLOTS, 0, SLOTS - 1)
    sender = row_of * N_COL + peer
    sent = send_blocks[sender, col_of, slot]
    live = slot < send_counts[sender, col_of]
    lower = block < BND
    inside = (block >= BND) & (block < BND + NBLK)
    upper = (block >= BND + NBLK) & (block < base)
    lower_dev = jnp.clip(row_of - 1, 0, N_ROW - 1) * N_COL + col_of
    upper_dev = jnp.clip(row_of + 1, 0, N_ROW - 1) * N_COL + col_of
    whole = jnp.where(lower, lower_dev * NBLK + NBLK - BND + block, jnp.where(inside, owner * NBLK + block - BND, jnp.where(upper, upper_dev * NBLK + block - BND - NBLK, sender * NBLK + sent)))
    valid = jnp.where(lower, row_of > 0, jnp.where(inside, True, jnp.where(upper, row_of < N_ROW - 1, live)))
    whole = jnp.where(valid, whole, 0).astype(jnp.int32)
    return ((whole * BLOCK + edge_nodes[:, 0]).astype(jnp.int32), valid, owner)

def reference(nodes, edge_feats, edge_blocks, edge_nodes, send_blocks, send_counts, edge_w1, edge_b1, edge_w2, edge_gain, node_w1, node_b1, node_w2, node_gain, node_cot, edge_cot):
    devices = N_ROW * N_COL
    source, valid, owner = source_rows(edge_blocks, edge_nodes, send_blocks, send_counts)
    target = (owner * (NBLK * BLOCK) + edge_blocks[:, 1] * BLOCK + edge_nodes[:, 1]).astype(jnp.int32)

    def shaped(array):
        return array.reshape((devices, E_DEV) + array.shape[1:])

    def edge_joined(src, present, tgt, feats):
        picked = nodes[src]
        picked = jnp.where(present[:, None], picked, jnp.zeros_like(picked))
        return jnp.concatenate([picked, nodes[tgt], feats], axis=1)

    def forward_one(pieces):
        src, present, tgt, feats = pieces
        out, saved = mlp_forward(edge_joined(src, present, tgt, feats), edge_w1, edge_b1, edge_w2, edge_gain)
        return out.astype(jnp.bfloat16)
    message = lax.map(forward_one, (shaped(source), shaped(valid), shaped(target), shaped(edge_feats)))
    message = message.reshape(devices * E_DEV, WIDTH)
    edge_new = (edge_feats.astype(jnp.float32) + message.astype(jnp.float32)).astype(jnp.bfloat16)
    summed = jax.ops.segment_sum(message.astype(jnp.float32), target, num_segments=NODES).astype(jnp.bfloat16)
    node_joined = jnp.concatenate([nodes, summed], axis=1)
    node_out, node_saved = mlp_forward(node_joined, node_w1, node_b1, node_w2, node_gain)
    node_new = (nodes.astype(jnp.float32) + node_out).astype(jnp.bfloat16)
    upstream = node_cot.astype(jnp.float32)
    d_node_joined, node_g1, node_g2 = mlp_backward(upstream, node_joined, node_saved, node_w1, node_w2, node_gain)
    d_summed = d_node_joined[:, WIDTH:]

    def backward_one(carry, pieces):
        node_acc, g_first, g_second = carry
        src, present, tgt, feats, cot_edge = pieces
        joined = edge_joined(src, present, tgt, feats)
        out, saved = mlp_forward(joined, edge_w1, edge_b1, edge_w2, edge_gain)
        d_message = d_summed[tgt] + cot_edge.astype(jnp.float32)
        d_joined, part_first, part_second = mlp_backward(d_message, joined, saved, edge_w1, edge_w2, edge_gain)
        d_source = jnp.where(present[:, None], d_joined[:, :WIDTH], 0.0)
        node_acc = node_acc.at[src].add(d_source).at[tgt].add(d_joined[:, WIDTH:2 * WIDTH])
        grad_edge = (cot_edge.astype(jnp.float32) + d_joined[:, 2 * WIDTH:]).astype(jnp.bfloat16)
        return ((node_acc, g_first + part_first, g_second + part_second), grad_edge)
    start = (upstream + d_node_joined[:, :WIDTH], jnp.zeros((3 * WIDTH, WIDTH), jnp.float32), jnp.zeros((WIDTH, WIDTH), jnp.float32))
    carry, edge_grad = lax.scan(backward_one, start, (shaped(source), shaped(valid), shaped(target), shaped(edge_feats), shaped(edge_cot)))
    node_grad, edge_g1, edge_g2 = carry
    edge_grad = edge_grad.reshape(devices * E_DEV, WIDTH)
    edge_scale = float(EDGES) ** (-0.5)
    node_scale = float(NODES) ** (-0.5)
    return (node_new, edge_new, node_grad, edge_grad, edge_g1 * edge_scale, edge_g2 * edge_scale, node_g1 * node_scale, node_g2 * node_scale)
```

```python
import jax
import jax.numpy as jnp
from jax import lax
from jax.experimental import pallas as pl
from jax.experimental.pallas import tpu as pltpu
from jax.sharding import Mesh, PartitionSpec as P

BLOCK = 128
W = 128
EPS = 1e-05
BF = jnp.bfloat16
F32 = jnp.float32

SPLIT = {"x": 4, "z": 12, "c": 2, "y": 8}
ALL = ("x", "z", "c", "y")
ROW = ("x", "z", "c")
SCATTER = ("x", "y")
SPREAD = ("z", "c")
CHUNK = 256
WROWS = 1024


def dot(a, b, dims=((1,), (0,))):
    return lax.dot_general(a, b, (dims, ((), ())), preferred_element_type=F32)


TN = ((0,), (0,))
NT = ((1,), (1,))


def full(shape):
    return pl.BlockSpec(shape, memory_space=pltpu.VMEM)


SMEM = pl.BlockSpec(memory_space=pltpu.SMEM)


def row_mean(v):
    return jnp.mean(v, axis=-1, keepdims=True)


def norm_rows(second):
    centred = second - row_mean(second)
    scale = lax.rsqrt(row_mean(centred * centred) + EPS)
    return centred * scale, scale


def norm_back(along, unit, scale):
    return scale * (along - row_mean(along) - unit * row_mean(along * unit))


def silu_parts(first):
    sig = jax.nn.sigmoid(first)
    return (first * sig).astype(BF), sig * (1.0 + first * (1.0 - sig))


def two_halves(v):
    high = v.astype(BF)
    low = (v - high.astype(F32)).astype(BF)
    return high, low


def marks(node, block, shape, dim):
    spot = lax.broadcasted_iota(jnp.int32, shape, dim).astype(F32)
    return jnp.where(node == spot, block, -1.0).astype(BF)


def one_hot(mark, block):
    return jnp.where(mark == block, 1.0, 0.0).astype(BF)


def pack_kernel(blocks, counts, nodes, out):
    for p in range(out.shape[0]):
        for s in range(out.shape[1] // BLOCK):
            at = pl.multiple_of(blocks[s, p] * BLOCK, BLOCK)
            live = jnp.where(s < counts[0, p], 1.0, 0.0).astype(BF)
            out[p, s * BLOCK : (s + 1) * BLOCK, :] = nodes[pl.ds(at, BLOCK), :] * live


def main_kernel(
    lower, upper, incoming, nodes, eb, en, feats, ecot, ncot,
    ew1, eb1, ew2, egain, nw1, nb1, nw2, ngain,
    node_new, edge_new, wsum, d_first_out, base,
    ext, cols, joined, active, unit, slope, scales, tmark, summed, dsum, g1, g2,
    *, edge_scale, node_scale,
):
    rows = feats.shape[0]
    nblk = nodes.shape[0] // BLOCK
    ext[0:BLOCK, :] = lower[...]
    ext[BLOCK : BLOCK + nblk * BLOCK, :] = nodes[...]
    top = BLOCK + nblk * BLOCK
    ext[top : top + BLOCK, :] = upper[...]
    ext[top + BLOCK :, :] = incoming[...]
    n_ext = ext.shape[0] // BLOCK
    index = jnp.concatenate([eb[...], en[...], eb[...], en[...]], axis=0).astype(F32)
    cols[...] = index.T
    summed[...] = jnp.zeros_like(summed)
    g1[...] = jnp.zeros_like(g1)
    g2[...] = jnp.zeros_like(g2)

    def forward(i, carry):
        at = pl.ds(pl.multiple_of(i * CHUNK, CHUNK), CHUNK)
        col = cols[at, :]
        smark = marks(col[:, 2:3], col[:, 0:1], (CHUNK, BLOCK), 1)
        hot = jnp.concatenate([one_hot(smark, b) for b in range(n_ext)], axis=1)
        joined[at, 0:W] = dot(hot, ext[...]).astype(BF)
        tm = marks(col[:, 3:4], col[:, 1:2], (CHUNK, BLOCK), 1)
        tmark[at, :] = tm
        hot_t = jnp.concatenate([one_hot(tm, b) for b in range(nblk)], axis=1)
        joined[at, W : 2 * W] = dot(hot_t, nodes[...]).astype(BF)
        feat = feats[at, :]
        joined[at, 2 * W : 3 * W] = feat
        first = dot(joined[at, :], ew1[...]) + eb1[...]
        act, slp = silu_parts(first)
        active[at, :] = act
        slope[at, :] = slp
        second = dot(act, ew2[...])
        u, s = norm_rows(second)
        unit[at, :] = u
        scales[at, :] = jnp.broadcast_to(s, (CHUNK, W))
        message = (u * egain[...]).astype(BF)
        edge_new[at, :] = (feat.astype(F32) + message.astype(F32)).astype(BF)
        summed[...] += dot(hot_t, message, TN)
        return carry

    lax.fori_loop(0, rows // CHUNK, forward, 0)

    joined_n = jnp.concatenate([nodes[...], summed[...].astype(BF)], axis=1)
    first = dot(joined_n, nw1[...]) + nb1[...]
    act, slp = silu_parts(first)
    u, s = norm_rows(dot(act, nw2[...]))
    node_new[...] = (nodes[...].astype(F32) + u * ngain[...]).astype(BF)
    upstream = ncot[...].astype(F32)
    d_second = norm_back(upstream * ngain[...], u, s).astype(BF)
    wsum[768:896, :] = (dot(act, d_second, TN) * node_scale).astype(BF)
    d_first = (dot(d_second, nw2[...], NT) * slp).astype(BF)
    wsum[512:768, :] = (dot(joined_n, d_first, TN) * node_scale).astype(BF)
    d_joined = dot(d_first, nw1[...], NT)
    base[...] = upstream + d_joined[:, 0:W]
    high, low = two_halves(d_joined[:, W:])
    dsum[:, 0:W] = high
    dsum[:, W:] = low

    def backward(i, carry):
        at = pl.ds(pl.multiple_of(i * CHUNK, CHUNK), CHUNK)
        tm = tmark[at, :]
        hot_t = jnp.concatenate([one_hot(tm, b) for b in range(nblk)], axis=1)
        both = dot(hot_t, dsum[...])
        d_message = both[:, 0:W] + both[:, W:] + ecot[at, :].astype(F32)
        d_second = norm_back(d_message * egain[...], unit[at, :], scales[at, :]).astype(BF)
        g2[...] += dot(active[at, :], d_second, TN)
        d_first = (dot(d_second, ew2[...], NT) * slope[at, :]).astype(BF)
        d_first_out[at, :] = d_first
        g1[...] += dot(joined[at, :], d_first, TN)
        return carry

    lax.fori_loop(0, rows // CHUNK, backward, 0)
    wsum[0:384, :] = (g1[...] * edge_scale).astype(BF)
    wsum[384:512, :] = (g2[...] * edge_scale).astype(BF)
    wsum[896:, :] = jnp.zeros_like(wsum[896:, :])


def back_kernel(eb, en, d_first, ecot, ew1, slots, to_lower, to_upper, own, target, edge_grad):
    rows = d_first.shape[0]
    d = d_first[...]
    nblk = own.shape[0] // BLOCK
    block = eb[...].astype(F32)
    node = en[...].astype(F32)
    smark = marks(node[0:1, :], block[0:1, :], (BLOCK, rows), 0)

    def part(b, count):
        return dot(jnp.concatenate([one_hot(smark, b + k) for k in range(count)], axis=0), d)

    for p in range(slots.shape[0]):
        slots[p] = part(nblk + 2 + 2 * p, 2).astype(BF)
    to_lower[...] = part(0, 1).astype(BF)
    to_upper[...] = part(nblk + 1, 1).astype(BF)
    own[...] = part(1, nblk)
    tmark = marks(node[1:2, :], block[1:2, :], (BLOCK, rows), 0)
    target[...] = dot(jnp.concatenate([one_hot(tmark, b) for b in range(nblk)], axis=0), d)
    edge_grad[...] = (ecot[...].astype(F32) + dot(d, ew1[2 * W :, :], NT)).astype(BF)


def finish_kernel(blocks, counts, slots, from_lower, from_upper, own, target, base, ew1, out, total):
    nblk = own.shape[0] // BLOCK
    total[...] = own[...]
    total[0:BLOCK, :] += from_lower[...].astype(F32)
    total[(nblk - 1) * BLOCK :, :] += from_upper[...].astype(F32)
    for p in range(slots.shape[0]):
        for s in range(slots.shape[1] // BLOCK):
            at = pl.ds(pl.multiple_of(blocks[s, p] * BLOCK, BLOCK), BLOCK)
            live = jnp.where(s < counts[0, p], 1.0, 0.0)
            total[at, :] += slots[p, s * BLOCK : (s + 1) * BLOCK, :].astype(F32) * live
    source_high, source_low = two_halves(total[...])
    target_high, target_low = two_halves(target[...])
    weights = ew1[...]
    out[...] = (
        base[...]
        + dot(source_high, weights[0:W, :], NT)
        + dot(source_low, weights[0:W, :], NT)
        + dot(target_high, weights[W : 2 * W, :], NT)
        + dot(target_low, weights[W : 2 * W, :], NT)
    )


def add_kernel(pieces, out):
    total = jnp.sum(pieces[...].astype(F32), axis=0).astype(BF)
    for k in range(out.shape[0]):
        out[k] = total


def exchange(value, axes):
    return lax.all_to_all(value, axes, split_axis=0, concat_axis=0, tiled=True)


def call(kernel, outs, scratch=(), in_specs=None, cost=None):
    return pl.pallas_call(
        kernel,
        out_shape=outs,
        in_specs=in_specs,
        out_specs=jax.tree.map(lambda o: pl.BlockSpec(memory_space=pltpu.VMEM), outs),
        scratch_shapes=scratch,
        compiler_params=pltpu.CompilerParams(vmem_limit_bytes=40 << 20),
        cost_estimate=cost,
    )


VM = pl.BlockSpec(memory_space=pltpu.VMEM)


def arr(shape, dtype):
    return jax.ShapeDtypeStruct(shape, dtype)


def local(
    nodes, edge_feats, edge_blocks, edge_nodes, send_blocks, send_counts,
    edge_w1, edge_b1, edge_w2, edge_gain, node_w1, node_b1, node_w2, node_gain,
    node_cot, edge_cot,
):
    own_rows = nodes.shape[0]
    edges = edge_feats.shape[0]
    n_col, slots = send_blocks.shape[1:]
    n_row = lax.axis_size(ROW)
    devices = n_row * n_col
    edge_scale = float(edges * devices) ** (-0.5)
    node_scale = float(own_rows * devices) ** (-0.5)
    blocks = send_blocks[0].T
    up = [(i, i + 1) for i in range(n_row - 1)]
    down = [(i + 1, i) for i in range(n_row - 1)]
    eb = edge_blocks.T
    en = edge_nodes.T

    outgoing = call(
        pack_kernel,
        arr((n_col, slots * BLOCK, W), BF),
        in_specs=[SMEM, SMEM, VM],
        cost=pl.CostEstimate(flops=0, bytes_accessed=600000, transcendentals=0),
    )(blocks, send_counts, nodes)
    incoming = exchange(outgoing, "y")
    lower = lax.ppermute(nodes[own_rows - BLOCK :], ROW, up)
    upper = lax.ppermute(nodes[:BLOCK], ROW, down)

    n_ext = own_rows + 2 * BLOCK + n_col * slots * BLOCK
    node_new, edge_new, wsum, d_first, base = call(
        lambda *refs: main_kernel(*refs, edge_scale=edge_scale, node_scale=node_scale),
        (
            arr((own_rows, W), BF),
            arr((edges, W), BF),
            arr((WROWS, W), BF),
            arr((edges, W), BF),
            arr((own_rows, W), F32),
        ),
        scratch=[
            pltpu.VMEM((n_ext, W), BF),
            pltpu.VMEM((edges, 8), F32),
            pltpu.VMEM((edges, 3 * W), BF),
            pltpu.VMEM((edges, W), BF),
            pltpu.VMEM((edges, W), F32),
            pltpu.VMEM((edges, W), F32),
            pltpu.VMEM((edges, W), F32),
            pltpu.VMEM((edges, W), BF),
            pltpu.VMEM((own_rows, W), F32),
            pltpu.VMEM((own_rows, 2 * W), BF),
            pltpu.VMEM((3 * W, W), F32),
            pltpu.VMEM((W, W), F32),
        ],
        in_specs=[VM] * 17,
        cost=pl.CostEstimate(flops=4 * 10**9, bytes_accessed=4000000, transcendentals=200000),
    )(
        lower, upper, incoming.reshape(n_col * slots * BLOCK, W), nodes, eb, en,
        edge_feats, edge_cot, node_cot,
        edge_w1, edge_b1[None], edge_w2, edge_gain[None],
        node_w1, node_b1[None], node_w2, node_gain[None],
    )

    members = lax.axis_size(SCATTER)
    share = WROWS // members
    pieces = exchange(wsum.reshape(members, share, W), SCATTER)
    spread = lax.axis_size(SPREAD)
    part = call(add_kernel, arr((spread, share, W), BF), in_specs=[VM])(pieces)
    pieces = exchange(part, SPREAD)
    part = call(add_kernel, arr((members, share, W), BF), in_specs=[VM])(pieces)
    weights = exchange(part, SCATTER)
    weights = weights.reshape(WROWS, W).astype(F32)

    slots_out, to_lower, to_upper, own, target, edge_grad = call(
        back_kernel,
        (
            arr((n_col, slots * BLOCK, W), BF),
            arr((BLOCK, W), BF),
            arr((BLOCK, W), BF),
            arr((own_rows, W), F32),
            arr((own_rows, W), F32),
            arr((edges, W), BF),
        ),
        in_specs=[VM] * 5,
        cost=pl.CostEstimate(flops=10**9, bytes_accessed=2000000, transcendentals=0),
    )(eb, en, d_first, edge_cot, edge_w1)
    slot_back = exchange(slots_out, "y")
    from_lower = lax.ppermute(to_upper, ROW, up)
    from_upper = lax.ppermute(to_lower, ROW, down)
    node_grad = call(
        finish_kernel,
        arr((own_rows, W), F32),
        scratch=[pltpu.VMEM((own_rows, W), F32)],
        in_specs=[SMEM, SMEM] + [VM] * 7,
        cost=pl.CostEstimate(flops=10**8, bytes_accessed=1000000, transcendentals=0),
    )(blocks, send_counts, slot_back, from_lower, from_upper, own, target, base, edge_w1)
    return (
        node_new,
        edge_new,
        node_grad,
        edge_grad,
        weights[0:384],
        weights[384:512],
        weights[512:768],
        weights[768:896],
    )


def solution(mesh):
    fine = Mesh(mesh.devices.reshape(tuple(SPLIT.values())), tuple(SPLIT))
    whole = P()
    owned = P(ALL)
    return jax.shard_map(
        local,
        mesh=fine,
        in_specs=(owned,) * 6 + (whole,) * 8 + (owned,) * 2,
        out_specs=(owned,) * 4 + (whole,) * 4,
        check_vma=False,
    )
```

```python
import jax
import jax.numpy as jnp
from jax import lax
from jax.experimental import pallas as pl
from jax.experimental.pallas import tpu as pltpu
from jax.sharding import Mesh, PartitionSpec as P

BLOCK = 128
W = 128
EPS = 1e-05
BF = jnp.bfloat16
F32 = jnp.float32

SPLIT = {"x": 4, "z": 12, "c": 2, "y": 8}
ALL = ("x", "z", "c", "y")
ROW = ("x", "z", "c")
SCATTER = ("x", "c", "y")
SPREAD = "z"
CHUNK = 256
WROWS = 1024
LABEL = 16


def dot(a, b, dims=((1,), (0,))):
    return lax.dot_general(a, b, (dims, ((), ())), preferred_element_type=F32)


TN = ((0,), (0,))
NT = ((1,), (1,))


def full(shape):
    return pl.BlockSpec(shape, memory_space=pltpu.VMEM)


SMEM = pl.BlockSpec(memory_space=pltpu.SMEM)


def row_mean(v):
    return jnp.mean(v, axis=-1, keepdims=True)


def norm_rows(second):
    centred = second - row_mean(second)
    scale = lax.rsqrt(row_mean(centred * centred) + EPS)
    return centred * scale, scale


def norm_back(along, unit, scale):
    return scale * (along - row_mean(along) - unit * row_mean(along * unit))


def silu_parts(first):
    sig = jax.nn.sigmoid(first)
    return (first * sig).astype(BF), sig * (1.0 + first * (1.0 - sig))


def two_halves(v):
    high = v.astype(BF)
    low = (v - high.astype(F32)).astype(BF)
    return high, low


def marks(node, block, shape, dim):
    spot = lax.broadcasted_iota(jnp.int32, shape, dim).astype(F32)
    return jnp.where(node == spot, block, -1.0).astype(BF)


def one_hot(mark, block):
    if not isinstance(block, int):
        block = jnp.full(mark.shape, block.astype(F32)).astype(BF)
    return jnp.where(mark == block, 1.0, 0.0).astype(BF)


def pack_kernel(blocks, counts, nodes, out):
    n_slots = blocks.shape[0]
    pair = n_slots * BLOCK
    spot = lax.broadcasted_iota(jnp.int32, (LABEL, W), 0)
    for p in range(out.shape[0]):
        label = jnp.zeros((LABEL, W), F32)
        for s in range(n_slots):
            at = pl.multiple_of(blocks[s, p] * BLOCK, BLOCK)
            live = jnp.where(s < counts[0, p], 1.0, 0.0).astype(BF)
            out[p, s * BLOCK : (s + 1) * BLOCK, :] = nodes[pl.ds(at, BLOCK), :] * live
            label = jnp.where(spot == s, blocks[s, p].astype(F32), label)
        out[p, pair:, :] = label.astype(BF)


def early_kernel(nodes, eb, en, feats, ew1, eb1, smark, upper_half, tmark, joined, partial, cols, *, half):
    rows = feats.shape[0]
    nblk = nodes.shape[0] // BLOCK
    index = jnp.concatenate([eb[...], en[...], eb[...], en[...]], axis=0).astype(F32)
    cols[...] = index.T

    def step(i, carry):
        at = pl.ds(pl.multiple_of(i * CHUNK, CHUNK), CHUNK)
        col = cols[at, :]
        block = col[:, 0:1]
        high = block >= half
        smark[at, :] = marks(col[:, 2:3], jnp.where(high, block - half, block), (CHUNK, BLOCK), 1)
        upper_half[at, :] = jnp.broadcast_to(jnp.where(high, 1.0, 0.0), (CHUNK, W)).astype(BF)
        tm = marks(col[:, 3:4], col[:, 1:2], (CHUNK, BLOCK), 1)
        tmark[at, :] = tm
        hot_t = jnp.concatenate([one_hot(tm, b) for b in range(nblk)], axis=1)
        joined[at, 0:W] = dot(hot_t, nodes[...]).astype(BF)
        joined[at, W : 2 * W] = feats[at, :]
        partial[at, :] = dot(joined[at, :], ew1[W:, :]) + eb1[...]
        return carry

    lax.fori_loop(0, rows // CHUNK, step, 0)


def main_kernel(
    lower, upper, incoming, nodes, eb, en, smark, upper_half, tmark, joined, partial, ecot, ncot,
    ew1, ew2, egain, nw1, nb1, nw2, ngain,
    node_new, edge_new, wsum, d_first_out, base,
    ext, gathered, active, unit, slope, scales, summed, dsum, g1, g2,
    *, edge_scale, node_scale,
):
    rows = joined.shape[0]
    nblk = nodes.shape[0] // BLOCK
    half = ext.shape[0] // BLOCK

    def place(b, block):
        at = (b % half) * BLOCK
        ext[at : at + BLOCK, (b // half) * W : (b // half + 1) * W] = block

    place(0, lower[...])
    for b in range(nblk):
        place(1 + b, nodes[b * BLOCK : (b + 1) * BLOCK, :])
    place(1 + nblk, upper[...])
    n_slots = 2 * (half - 1) // incoming.shape[0]
    for p in range(incoming.shape[0]):
        for k in range(n_slots):
            place(2 + nblk + n_slots * p + k, incoming[p, k * BLOCK : (k + 1) * BLOCK, :])
    summed[...] = jnp.zeros_like(summed)
    g1[...] = jnp.zeros_like(g1)
    g2[...] = jnp.zeros_like(g2)

    def target_hot(at):
        tm = tmark[at, :]
        return jnp.concatenate([one_hot(tm, b) for b in range(nblk)], axis=1)

    def forward(i, carry):
        at = pl.ds(pl.multiple_of(i * CHUNK, CHUNK), CHUNK)
        sm = smark[at, :]
        hot = jnp.concatenate([one_hot(sm, b) for b in range(half)], axis=1)
        both = dot(hot, ext[...])
        source = jnp.where(upper_half[at, :].astype(F32) > 0.5, both[:, W:], both[:, 0:W]).astype(BF)
        gathered[at, :] = source
        act, slp = silu_parts(partial[at, :] + dot(source, ew1[0:W, :]))
        active[at, :] = act
        slope[at, :] = slp
        u, s = norm_rows(dot(act, ew2[...]))
        unit[at, :] = u
        scales[at, :] = jnp.broadcast_to(s, (CHUNK, W))
        message = (u * egain[...]).astype(BF)
        edge_new[at, :] = (joined[at, W:].astype(F32) + message.astype(F32)).astype(BF)
        row = marks(en[1:2, at].astype(F32), eb[1:2, at].astype(F32), (BLOCK, CHUNK), 0)
        hot_row = jnp.concatenate([one_hot(row, b) for b in range(nblk)], axis=0)
        summed[...] += dot(hot_row, message)
        return carry

    lax.fori_loop(0, rows // CHUNK, forward, 0)

    joined_n = jnp.concatenate([nodes[...], summed[...].astype(BF)], axis=1)
    first = dot(joined_n, nw1[...]) + nb1[...]
    act, slp = silu_parts(first)
    u, s = norm_rows(dot(act, nw2[...]))
    node_new[...] = (nodes[...].astype(F32) + u * ngain[...]).astype(BF)
    upstream = ncot[...].astype(F32)
    d_second = norm_back(upstream * ngain[...], u, s).astype(BF)
    wsum[768:896, :] = (dot(act, d_second, TN) * node_scale).astype(BF)
    d_first = (dot(d_second, nw2[...], NT) * slp).astype(BF)
    wsum[512:768, :] = (dot(joined_n, d_first, TN) * node_scale).astype(BF)
    d_joined = dot(d_first, nw1[...], NT)
    base[...] = upstream + d_joined[:, 0:W]
    high, low = two_halves(d_joined[:, W:])
    dsum[:, 0:W] = high
    dsum[:, W:] = low

    def backward(i, carry):
        at = pl.ds(pl.multiple_of(i * CHUNK, CHUNK), CHUNK)
        both = dot(target_hot(at), dsum[...])
        d_message = both[:, 0:W] + both[:, W:] + ecot[at, :].astype(F32)
        d_second = norm_back(d_message * egain[...], unit[at, :], scales[at, :]).astype(BF)
        g2[...] += dot(d_second, active[at, :], TN)
        d_first = (dot(d_second, ew2[...], NT) * slope[at, :]).astype(BF)
        d_first_out[at, :] = d_first
        sources = jnp.concatenate([gathered[at, :], joined[at, :]], axis=1)
        g1[...] += dot(d_first, sources, TN)
        return carry

    lax.fori_loop(0, rows // CHUNK, backward, 0)
    wsum[0:384, :] = (g1[...].T * edge_scale).astype(BF)
    wsum[384:512, :] = (g2[...].T * edge_scale).astype(BF)
    wsum[896:, :] = jnp.zeros_like(wsum[896:, :])


def back_kernel(
    me, eb, en, incoming, d_first, ecot, ew1,
    far, near, to_lower, to_upper, own, target, edge_grad,
):
    rows = d_first.shape[0]
    d = d_first[...]
    nblk = own.shape[0] // BLOCK
    peers, n_slots = incoming.shape[0], incoming.shape[1] // BLOCK
    names = n_slots * BLOCK
    rim_blocks = nblk + 2
    block = eb[0:1, :].astype(F32)
    node = en[...].astype(F32)
    owned = block
    for p in range(peers):
        for s in range(n_slots):
            there = incoming[p, names + s : names + s + 1, 0:1].astype(F32) + float(rim_blocks + nblk * p)
            owned = jnp.where(block == float(rim_blocks + n_slots * p + s), there, owned)
    smark = marks(node[0:1, :], owned, (BLOCK, rows), 0)

    def part(b, count):
        return dot(jnp.concatenate([one_hot(smark, b + k) for k in range(count)], axis=0), d)

    for place in range(peers):
        sums = part(rim_blocks + nblk * (me[0] ^ place), nblk)
        if place < peers // 2:
            near[place] = sums
        else:
            far[place - peers // 2] = sums.astype(BF)
    to_lower[...] = part(0, 1).astype(BF)
    to_upper[...] = part(nblk + 1, 1).astype(BF)
    own[...] = part(1, nblk)
    tmark = marks(node[1:2, :], eb[1:2, :].astype(F32), (BLOCK, rows), 0)
    target[...] = dot(jnp.concatenate([one_hot(tmark, b) for b in range(nblk)], axis=0), d)
    edge_grad[...] = (ecot[...].astype(F32) + dot(d, ew1[2 * W :, :], NT)).astype(BF)


def fold_kernel(*refs):
    near, arrived, keep, send = refs[-4:]
    count = keep.shape[0]
    for k in range(2 * count):
        total = near[k] + arrived[k].astype(F32)
        if k < count:
            keep[k] = total
        else:
            send[k - count] = total.astype(BF)


def finish_kernel(near, arrived, from_lower, from_upper, own, target, base, ew1, out, total):
    nblk = own.shape[0] // BLOCK
    total[...] = own[...] + near[0] + arrived[0].astype(F32)
    total[0:BLOCK, :] += from_lower[...].astype(F32)
    total[(nblk - 1) * BLOCK :, :] += from_upper[...].astype(F32)
    source_high, source_low = two_halves(total[...])
    target_high, target_low = two_halves(target[...])
    weights = ew1[...]
    out[...] = (
        base[...]
        + dot(source_high, weights[0:W, :], NT)
        + dot(source_low, weights[0:W, :], NT)
        + dot(target_high, weights[W : 2 * W, :], NT)
        + dot(target_low, weights[W : 2 * W, :], NT)
    )


def unpack_kernel(weights, *outs):
    at = 0
    share = weights.shape[1]
    for out in outs:
        for k in range(out.shape[0] // share):
            out[k * share : (k + 1) * share, :] = weights[at].astype(F32)
            at += 1


def add_kernel(pieces, out):
    total = jnp.sum(pieces[...].astype(F32), axis=0).astype(BF)
    for k in range(out.shape[0]):
        out[k] = total


def exchange(value, axes):
    return lax.all_to_all(value, axes, split_axis=0, concat_axis=0, tiled=True)


def swap(value, bit):
    return lax.ppermute(value, "y", [(i, i ^ bit) for i in range(lax.axis_size("y"))])


def fold(after, near, arrived):
    some = [pl.BlockSpec(memory_space=pl.ANY)] * len(after)
    count, *rest = near.shape
    return call(
        fold_kernel,
        (arr((count // 2, *rest), F32), arr((count // 2, *rest), BF)),
        in_specs=some + [VM, VM],
    )(*after, near, arrived)


def call(kernel, outs, scratch=(), in_specs=None, cost=None):
    return pl.pallas_call(
        kernel,
        out_shape=outs,
        in_specs=in_specs,
        out_specs=jax.tree.map(lambda o: pl.BlockSpec(memory_space=pltpu.VMEM), outs),
        scratch_shapes=scratch,
        compiler_params=pltpu.CompilerParams(vmem_limit_bytes=60 << 20),
        cost_estimate=cost,
    )


VM = pl.BlockSpec(memory_space=pltpu.VMEM)


def arr(shape, dtype):
    return jax.ShapeDtypeStruct(shape, dtype)


def local(
    nodes, edge_feats, edge_blocks, edge_nodes, send_blocks, send_counts,
    edge_w1, edge_b1, edge_w2, edge_gain, node_w1, node_b1, node_w2, node_gain,
    node_cot, edge_cot,
):
    own_rows = nodes.shape[0]
    edges = edge_feats.shape[0]
    n_col, slots = send_blocks.shape[1:]
    n_row = lax.axis_size(ROW)
    devices = n_row * n_col
    edge_scale = float(edges * devices) ** (-0.5)
    node_scale = float(own_rows * devices) ** (-0.5)
    blocks = send_blocks[0].T
    up = [(i, i + 1) for i in range(n_row - 1)]
    down = [(i + 1, i) for i in range(n_row - 1)]
    eb = edge_blocks.T
    en = edge_nodes.T

    outgoing = call(
        pack_kernel,
        arr((n_col, slots * BLOCK + LABEL, W), BF),
        in_specs=[SMEM, SMEM, VM],
        cost=pl.CostEstimate(flops=0, bytes_accessed=600000, transcendentals=0),
    )(blocks, send_counts, nodes)
    incoming = exchange(outgoing, "y")
    lower = lax.ppermute(nodes[own_rows - BLOCK :], ROW, up)
    upper = lax.ppermute(nodes[:BLOCK], ROW, down)

    n_ext = own_rows + 2 * BLOCK + n_col * slots * BLOCK
    smark, upper_half, tmark, joined, partial = call(
        lambda *refs: early_kernel(*refs, half=n_ext // BLOCK // 2),
        (
            arr((edges, W), BF),
            arr((edges, W), BF),
            arr((edges, W), BF),
            arr((edges, 2 * W), BF),
            arr((edges, W), F32),
        ),
        scratch=[pltpu.VMEM((edges, 8), F32)],
        in_specs=[VM] * 6,
        cost=pl.CostEstimate(flops=2 * 10**8, bytes_accessed=8000000, transcendentals=0),
    )(nodes, eb, en, edge_feats, edge_w1, edge_b1[None])
    node_new, edge_new, wsum, d_first, base = call(
        lambda *refs: main_kernel(*refs, edge_scale=edge_scale, node_scale=node_scale),
        (
            arr((own_rows, W), BF),
            arr((edges, W), BF),
            arr((WROWS, W), BF),
            arr((edges, W), BF),
            arr((own_rows, W), F32),
        ),
        scratch=[
            pltpu.VMEM((n_ext // 2, 2 * W), BF),
            pltpu.VMEM((edges, W), BF),
            pltpu.VMEM((edges, W), BF),
            pltpu.VMEM((edges, W), F32),
            pltpu.VMEM((edges, W), F32),
            pltpu.VMEM((edges, W), F32),
            pltpu.VMEM((own_rows, W), F32),
            pltpu.VMEM((own_rows, 2 * W), BF),
            pltpu.VMEM((W, 3 * W), F32),
            pltpu.VMEM((W, W), F32),
        ],
        in_specs=[VM] * 20,
        cost=pl.CostEstimate(flops=4 * 10**9, bytes_accessed=4000000, transcendentals=200000),
    )(
        lower, upper, incoming, nodes, eb, en, smark, upper_half, tmark,
        joined, partial, edge_cot, node_cot,
        edge_w1, edge_w2, edge_gain[None], node_w1, node_b1[None], node_w2, node_gain[None],
    )

    members = lax.axis_size(SCATTER)
    share = WROWS // members
    spread = lax.axis_size(SPREAD)
    pieces = exchange(wsum.reshape(members, share, W), SCATTER)

    me = lax.axis_index("y").astype(jnp.int32)[None]
    far, near, to_lower, to_upper, own, target, edge_grad = call(
        back_kernel,
        (
            arr((n_col // 2, own_rows, W), BF),
            arr((n_col // 2, own_rows, W), F32),
            arr((BLOCK, W), BF),
            arr((BLOCK, W), BF),
            arr((own_rows, W), F32),
            arr((own_rows, W), F32),
            arr((edges, W), BF),
        ),
        in_specs=[SMEM] + [VM] * 6,
        cost=pl.CostEstimate(flops=10**9, bytes_accessed=2000000, transcendentals=0),
    )(me, eb, en, incoming, d_first, edge_cot, edge_w1)
    far = swap(far, 4)
    from_lower = lax.ppermute(to_upper, ROW, up)
    from_upper = lax.ppermute(to_lower, ROW, down)

    part = call(add_kernel, arr((spread, share, W), BF), in_specs=[VM])(pieces)
    pieces = exchange(part, SPREAD)
    near, far = fold((part,), near, far)
    far = swap(far, 2)
    part = call(add_kernel, arr((members, share, W), BF), in_specs=[VM])(pieces)
    weights = exchange(part, SCATTER)
    near, far = fold((part, from_lower, from_upper), near, far)
    far = swap(far, 1)
    node_grad = call(
        finish_kernel,
        arr((own_rows, W), F32),
        scratch=[pltpu.VMEM((own_rows, W), F32)],
        in_specs=[VM] * 8,
        cost=pl.CostEstimate(flops=10**8, bytes_accessed=1000000, transcendentals=0),
    )(near, far, from_lower, from_upper, own, target, base, edge_w1)
    grads = call(
        unpack_kernel,
        tuple(arr((rows, W), F32) for rows in (3 * W, W, 2 * W, W)),
        in_specs=[VM],
    )(weights)
    return (node_new, edge_new, node_grad, edge_grad) + tuple(grads)


def solution(mesh):
    fine = Mesh(mesh.devices.reshape(tuple(SPLIT.values())), tuple(SPLIT))
    whole = P()
    owned = P(ALL)
    return jax.shard_map(
        local,
        mesh=fine,
        in_specs=(owned,) * 6 + (whole,) * 8 + (owned,) * 2,
        out_specs=(owned,) * 4 + (whole,) * 4,
        check_vma=False,
    )
```

```python
import jax
import jax.numpy as jnp
from jax import lax
from jax.experimental import pallas as pl
from jax.experimental.pallas import tpu as pltpu
from jax.sharding import Mesh, PartitionSpec as P

BLOCK = 128
W = 128
EPS = 1e-05
BF = jnp.bfloat16
F32 = jnp.float32

SPLIT = {"x": 4, "z": 12, "c": 2, "y": 8}
ALL = ("x", "z", "c", "y")
ROW = ("x", "z", "c")
SCATTER = ("x", "c", "y")
SPREAD = "z"
CHUNK = 256
WROWS = 1024
LABEL = 16


def dot(a, b, dims=((1,), (0,))):
    return lax.dot_general(a, b, (dims, ((), ())), preferred_element_type=F32)


TN = ((0,), (0,))
NT = ((1,), (1,))


def full(shape):
    return pl.BlockSpec(shape, memory_space=pltpu.VMEM)


SMEM = pl.BlockSpec(memory_space=pltpu.SMEM)


def row_mean(v):
    return jnp.mean(v, axis=-1, keepdims=True)


def norm_rows(second):
    centred = second - row_mean(second)
    scale = lax.rsqrt(row_mean(centred * centred) + EPS)
    return centred * scale, scale


def norm_back(along, unit, scale):
    return scale * (along - row_mean(along) - unit * row_mean(along * unit))


def silu_parts(first):
    sig = jax.nn.sigmoid(first)
    return (first * sig).astype(BF), sig * (1.0 + first * (1.0 - sig))


def two_halves(v):
    high = v.astype(BF)
    low = (v - high.astype(F32)).astype(BF)
    return high, low


def marks(node, block, shape, dim):
    spot = lax.broadcasted_iota(jnp.int32, shape, dim).astype(F32)
    return jnp.where(node == spot, block, -1.0).astype(BF)


def one_hot(mark, block):
    if not isinstance(block, int):
        block = jnp.full(mark.shape, block.astype(F32)).astype(BF)
    return jnp.where(mark == block, 1.0, 0.0).astype(BF)


def place_of(away):
    return ((away & 1) << 2) | (away & 2) | (away >> 2)


def pack_kernel(blocks, counts, nodes, out):
    n_slots = blocks.shape[0]
    pair = n_slots * BLOCK
    spot = lax.broadcasted_iota(jnp.int32, (LABEL, W), 0)
    for p in range(out.shape[0]):
        label = jnp.zeros((LABEL, W), F32)
        for s in range(n_slots):
            at = pl.multiple_of(blocks[s, p] * BLOCK, BLOCK)
            live = jnp.where(s < counts[0, p], 1.0, 0.0).astype(BF)
            out[p, s * BLOCK : (s + 1) * BLOCK, :] = nodes[pl.ds(at, BLOCK), :] * live
            label = jnp.where(spot == s, blocks[s, p].astype(F32), label)
        out[p, pair:, :] = label.astype(BF)


def early_kernel(nodes, eb, en, feats, ew1, eb1, smark, upper_half, tmark, joined, partial, cols, *, half):
    rows = feats.shape[0]
    nblk = nodes.shape[0] // BLOCK
    index = jnp.concatenate([eb[...], en[...], eb[...], en[...]], axis=0).astype(F32)
    cols[...] = index.T

    def step(i, carry):
        at = pl.ds(pl.multiple_of(i * CHUNK, CHUNK), CHUNK)
        col = cols[at, :]
        block = col[:, 0:1]
        high = block >= half
        smark[at, :] = marks(col[:, 2:3], jnp.where(high, block - half, block), (CHUNK, BLOCK), 1)
        upper_half[at, :] = jnp.broadcast_to(jnp.where(high, 1.0, 0.0), (CHUNK, W)).astype(BF)
        tm = marks(col[:, 3:4], col[:, 1:2], (CHUNK, BLOCK), 1)
        tmark[at, :] = tm
        hot_t = jnp.concatenate([one_hot(tm, b) for b in range(nblk)], axis=1)
        joined[at, 0:W] = dot(hot_t, nodes[...]).astype(BF)
        joined[at, W : 2 * W] = feats[at, :]
        partial[at, :] = dot(joined[at, :], ew1[W:, :]) + eb1[...]
        return carry

    lax.fori_loop(0, rows // CHUNK, step, 0)


def main_kernel(
    lower, upper, incoming, nodes, eb, en, smark, upper_half, tmark, joined, partial, ecot, ncot,
    ew1, ew2, egain, nw1, nb1, nw2, ngain,
    node_new, edge_new, wsum, d_first_out, base,
    ext, gathered, active, unit, slope, scales, summed, dsum, g1, g2,
    *, edge_scale, node_scale,
):
    rows = joined.shape[0]
    nblk = nodes.shape[0] // BLOCK
    half = ext.shape[0] // BLOCK

    def place(b, block):
        at = (b % half) * BLOCK
        ext[at : at + BLOCK, (b // half) * W : (b // half + 1) * W] = block

    place(0, lower[...])
    for b in range(nblk):
        place(1 + b, nodes[b * BLOCK : (b + 1) * BLOCK, :])
    place(1 + nblk, upper[...])
    n_slots = 2 * (half - 1) // incoming.shape[0]
    for p in range(incoming.shape[0]):
        for k in range(n_slots):
            place(2 + nblk + n_slots * p + k, incoming[p, k * BLOCK : (k + 1) * BLOCK, :])
    summed[...] = jnp.zeros_like(summed)
    g1[...] = jnp.zeros_like(g1)
    g2[...] = jnp.zeros_like(g2)

    def target_hot(at):
        tm = tmark[at, :]
        return jnp.concatenate([one_hot(tm, b) for b in range(nblk)], axis=1)

    def forward(i, carry):
        at = pl.ds(pl.multiple_of(i * CHUNK, CHUNK), CHUNK)
        sm = smark[at, :]
        hot = jnp.concatenate([one_hot(sm, b) for b in range(half)], axis=1)
        both = dot(hot, ext[...])
        source = jnp.where(upper_half[at, :].astype(F32) > 0.5, both[:, W:], both[:, 0:W]).astype(BF)
        gathered[at, :] = source
        act, slp = silu_parts(partial[at, :] + dot(source, ew1[0:W, :]))
        active[at, :] = act
        slope[at, :] = slp
        u, s = norm_rows(dot(act, ew2[...]))
        unit[at, :] = u
        scales[at, :] = jnp.broadcast_to(s, (CHUNK, W))
        message = (u * egain[...]).astype(BF)
        edge_new[at, :] = (joined[at, W:].astype(F32) + message.astype(F32)).astype(BF)
        row = marks(en[1:2, at].astype(F32), eb[1:2, at].astype(F32), (BLOCK, CHUNK), 0)
        hot_row = jnp.concatenate([one_hot(row, b) for b in range(nblk)], axis=0)
        summed[...] += dot(hot_row, message)
        return carry

    lax.fori_loop(0, rows // CHUNK, forward, 0)

    joined_n = jnp.concatenate([nodes[...], summed[...].astype(BF)], axis=1)
    first = dot(joined_n, nw1[...]) + nb1[...]
    act, slp = silu_parts(first)
    u, s = norm_rows(dot(act, nw2[...]))
    node_new[...] = (nodes[...].astype(F32) + u * ngain[...]).astype(BF)
    upstream = ncot[...].astype(F32)
    d_second = norm_back(upstream * ngain[...], u, s).astype(BF)
    wsum[768:896, :] = (dot(act, d_second, TN) * node_scale).astype(BF)
    d_first = (dot(d_second, nw2[...], NT) * slp).astype(BF)
    wsum[512:768, :] = (dot(joined_n, d_first, TN) * node_scale).astype(BF)
    d_joined = dot(d_first, nw1[...], NT)
    base[...] = upstream + d_joined[:, 0:W]
    high, low = two_halves(d_joined[:, W:])
    dsum[:, 0:W] = high
    dsum[:, W:] = low

    def backward(i, carry):
        at = pl.ds(pl.multiple_of(i * CHUNK, CHUNK), CHUNK)
        both = dot(target_hot(at), dsum[...])
        d_message = both[:, 0:W] + both[:, W:] + ecot[at, :].astype(F32)
        d_second = norm_back(d_message * egain[...], unit[at, :], scales[at, :]).astype(BF)
        g2[...] += dot(d_second, active[at, :], TN)
        d_first = (dot(d_second, ew2[...], NT) * slope[at, :]).astype(BF)
        d_first_out[at, :] = d_first
        sources = jnp.concatenate([gathered[at, :], joined[at, :]], axis=1)
        g1[...] += dot(d_first, sources, TN)
        return carry

    lax.fori_loop(0, rows // CHUNK, backward, 0)
    wsum[0:384, :] = (g1[...].T * edge_scale).astype(BF)
    wsum[384:512, :] = (g2[...].T * edge_scale).astype(BF)
    wsum[896:, :] = jnp.zeros_like(wsum[896:, :])


def back_kernel(
    me, eb, en, upper_half, incoming, d_first, ecot, ew1,
    far, near, to_lower, to_upper, own, target, edge_grad,
    wide, places, *, half,
):
    rows = d_first.shape[0]
    d = d_first[...]
    nblk = own.shape[0] // BLOCK
    peers, n_slots = incoming.shape[0], incoming.shape[1] // BLOCK
    names = n_slots * BLOCK
    rim_blocks = nblk + 2
    block = eb[0:1, :].astype(F32)
    node = en[...].astype(F32)
    owned = block
    for p in range(peers):
        for s in range(n_slots):
            there = incoming[p, names + s : names + s + 1, 0:1].astype(F32)
            there = there + float(rim_blocks + nblk * p)
            owned = jnp.where(block == float(rim_blocks + n_slots * p + s), there, owned)
    owned = jnp.where(owned >= half, owned - half, owned)
    smark = marks(node[0:1, :], owned, (BLOCK, rows), 0)
    high = d * upper_half[...]
    wide[:, 0:W] = d - high
    wide[:, W:] = high

    def store(b, sums):
        if b == 0:
            to_lower[...] = sums.astype(BF)
        elif b <= nblk:
            own[(b - 1) * BLOCK : b * BLOCK, :] = sums
        elif b == nblk + 1:
            to_upper[...] = sums.astype(BF)
        else:
            q, j = divmod(b - rim_blocks, nblk)
            places[place_of(q ^ me[0]), j * BLOCK : (j + 1) * BLOCK, :] = sums

    for b in range(0, half, 2):
        sums = dot(jnp.concatenate([one_hot(smark, b), one_hot(smark, b + 1)], axis=0), wide[...])
        for k in range(2):
            store(b + k, sums[k * BLOCK : (k + 1) * BLOCK, 0:W])
            store(b + k + half, sums[k * BLOCK : (k + 1) * BLOCK, W:])
    for place in range(peers):
        if place < peers // 2:
            near[place] = places[place]
        else:
            far[place - peers // 2] = places[place].astype(BF)
    tmark = marks(node[1:2, :], eb[1:2, :].astype(F32), (BLOCK, rows), 0)
    target[...] = dot(jnp.concatenate([one_hot(tmark, b) for b in range(nblk)], axis=0), d)
    edge_grad[...] = (ecot[...].astype(F32) + dot(d, ew1[2 * W :, :], NT)).astype(BF)


def fold_kernel(*refs):
    near, arrived, keep, send = refs[-4:]
    count = keep.shape[0]
    for k in range(2 * count):
        total = near[k] + arrived[k].astype(F32)
        if k < count:
            keep[k] = total
        else:
            send[k - count] = total.astype(BF)


def finish_kernel(near, arrived, from_lower, from_upper, own, target, base, ew1, out, total):
    nblk = own.shape[0] // BLOCK
    total[...] = own[...] + near[0] + arrived[0].astype(F32)
    total[0:BLOCK, :] += from_lower[...].astype(F32)
    total[(nblk - 1) * BLOCK :, :] += from_upper[...].astype(F32)
    source_high, source_low = two_halves(total[...])
    target_high, target_low = two_halves(target[...])
    weights = ew1[...]
    out[...] = (
        base[...]
        + dot(source_high, weights[0:W, :], NT)
        + dot(source_low, weights[0:W, :], NT)
        + dot(target_high, weights[W : 2 * W, :], NT)
        + dot(target_low, weights[W : 2 * W, :], NT)
    )


def unpack_kernel(weights, *outs):
    at = 0
    share = weights.shape[1]
    for out in outs:
        for k in range(out.shape[0] // share):
            out[k * share : (k + 1) * share, :] = weights[at].astype(F32)
            at += 1


def add_kernel(after, pieces, out):
    total = jnp.sum(pieces[...].astype(F32), axis=0).astype(BF)
    for k in range(out.shape[0]):
        out[k] = total


def exchange(value, axes):
    return lax.all_to_all(value, axes, split_axis=0, concat_axis=0, tiled=True)


def swap(value, bit):
    return lax.ppermute(value, "y", [(i, i ^ bit) for i in range(lax.axis_size("y"))])


def add(pieces, copies, after):
    return call(
        add_kernel,
        arr((copies,) + pieces.shape[1:], BF),
        in_specs=[pl.BlockSpec(memory_space=pl.ANY), VM],
    )(after, pieces)


def fold(after, near, arrived):
    some = [pl.BlockSpec(memory_space=pl.ANY)] * len(after)
    count, *rest = near.shape
    return call(
        fold_kernel,
        (arr((count // 2, *rest), F32), arr((count // 2, *rest), BF)),
        in_specs=some + [VM, VM],
    )(*after, near, arrived)


def call(kernel, outs, scratch=(), in_specs=None, cost=None):
    return pl.pallas_call(
        kernel,
        out_shape=outs,
        in_specs=in_specs,
        out_specs=jax.tree.map(lambda o: pl.BlockSpec(memory_space=pltpu.VMEM), outs),
        scratch_shapes=scratch,
        compiler_params=pltpu.CompilerParams(vmem_limit_bytes=24 << 20),
        cost_estimate=cost,
    )


VM = pl.BlockSpec(memory_space=pltpu.VMEM)


def arr(shape, dtype):
    return jax.ShapeDtypeStruct(shape, dtype)


def local(
    nodes, edge_feats, edge_blocks, edge_nodes, send_blocks, send_counts,
    edge_w1, edge_b1, edge_w2, edge_gain, node_w1, node_b1, node_w2, node_gain,
    node_cot, edge_cot,
):
    own_rows = nodes.shape[0]
    edges = edge_feats.shape[0]
    n_col, slots = send_blocks.shape[1:]
    n_row = lax.axis_size(ROW)
    devices = n_row * n_col
    edge_scale = float(edges * devices) ** (-0.5)
    node_scale = float(own_rows * devices) ** (-0.5)
    blocks = send_blocks[0].T
    up = [(i, i + 1) for i in range(n_row - 1)]
    down = [(i + 1, i) for i in range(n_row - 1)]
    eb = edge_blocks.T
    en = edge_nodes.T

    outgoing = call(
        pack_kernel,
        arr((n_col, slots * BLOCK + LABEL, W), BF),
        in_specs=[SMEM, SMEM, VM],
        cost=pl.CostEstimate(flops=0, bytes_accessed=600000, transcendentals=0),
    )(blocks, send_counts, nodes)
    incoming = exchange(outgoing, "y")
    lower = lax.ppermute(nodes[own_rows - BLOCK :], ROW, up)
    upper = lax.ppermute(nodes[:BLOCK], ROW, down)

    n_ext = own_rows + 2 * BLOCK + n_col * slots * BLOCK
    smark, upper_half, tmark, joined, partial = call(
        lambda *refs: early_kernel(*refs, half=n_ext // BLOCK // 2),
        (
            arr((edges, W), BF),
            arr((edges, W), BF),
            arr((edges, W), BF),
            arr((edges, 2 * W), BF),
            arr((edges, W), F32),
        ),
        scratch=[pltpu.VMEM((edges, 8), F32)],
        in_specs=[VM] * 6,
        cost=pl.CostEstimate(flops=2 * 10**8, bytes_accessed=8000000, transcendentals=0),
    )(nodes, eb, en, edge_feats, edge_w1, edge_b1[None])
    node_new, edge_new, wsum, d_first, base = call(
        lambda *refs: main_kernel(*refs, edge_scale=edge_scale, node_scale=node_scale),
        (
            arr((own_rows, W), BF),
            arr((edges, W), BF),
            arr((WROWS, W), BF),
            arr((edges, W), BF),
            arr((own_rows, W), F32),
        ),
        scratch=[
            pltpu.VMEM((n_ext // 2, 2 * W), BF),
            pltpu.VMEM((edges, W), BF),
            pltpu.VMEM((edges, W), BF),
            pltpu.VMEM((edges, W), F32),
            pltpu.VMEM((edges, W), F32),
            pltpu.VMEM((edges, W), F32),
            pltpu.VMEM((own_rows, W), F32),
            pltpu.VMEM((own_rows, 2 * W), BF),
            pltpu.VMEM((W, 3 * W), F32),
            pltpu.VMEM((W, W), F32),
        ],
        in_specs=[VM] * 20,
        cost=pl.CostEstimate(flops=4 * 10**9, bytes_accessed=4000000, transcendentals=200000),
    )(
        lower, upper, incoming, nodes, eb, en, smark, upper_half, tmark,
        joined, partial, edge_cot, node_cot,
        edge_w1, edge_w2, edge_gain[None], node_w1, node_b1[None], node_w2, node_gain[None],
    )

    members = lax.axis_size(SCATTER)
    share = WROWS // members
    spread = lax.axis_size(SPREAD)
    pieces = exchange(wsum.reshape(members, share, W), SCATTER)

    me = lax.axis_index("y").astype(jnp.int32)[None]
    far, near, to_lower, to_upper, own, target, edge_grad = call(
        lambda *refs: back_kernel(*refs, half=n_ext // BLOCK // 2),
        (
            arr((n_col // 2, own_rows, W), BF),
            arr((n_col // 2, own_rows, W), F32),
            arr((BLOCK, W), BF),
            arr((BLOCK, W), BF),
            arr((own_rows, W), F32),
            arr((own_rows, W), F32),
            arr((edges, W), BF),
        ),
        scratch=[pltpu.VMEM((edges, 2 * W), BF), pltpu.VMEM((n_col, own_rows, W), F32)],
        in_specs=[SMEM] + [VM] * 7,
        cost=pl.CostEstimate(flops=10**9, bytes_accessed=2000000, transcendentals=0),
    )(me, eb, en, upper_half, incoming, d_first, edge_cot, edge_w1)
    far = swap(far, 1)
    from_lower = lax.ppermute(to_upper, ROW, up)
    from_upper = lax.ppermute(to_lower, ROW, down)

    part = add(pieces, spread, far)
    pieces = exchange(part, SPREAD)
    near, far = fold((part,), near, far)
    far = swap(far, 2)
    part = add(pieces, members, far)
    weights = exchange(part, SCATTER)
    near, far = fold((part,), near, far)
    far = swap(far, 4)
    node_grad = call(
        finish_kernel,
        arr((own_rows, W), F32),
        scratch=[pltpu.VMEM((own_rows, W), F32)],
        in_specs=[VM] * 8,
        cost=pl.CostEstimate(flops=10**8, bytes_accessed=1000000, transcendentals=0),
    )(near, far, from_lower, from_upper, own, target, base, edge_w1)
    grads = call(
        unpack_kernel,
        tuple(arr((rows, W), F32) for rows in (3 * W, W, 2 * W, W)),
        in_specs=[VM],
    )(weights)
    return (node_new, edge_new, node_grad, edge_grad) + tuple(grads)


def solution(mesh):
    fine = Mesh(mesh.devices.reshape(tuple(SPLIT.values())), tuple(SPLIT))
    whole = P()
    owned = P(ALL)
    return jax.shard_map(
        local,
        mesh=fine,
        in_specs=(owned,) * 6 + (whole,) * 8 + (owned,) * 2,
        out_specs=(owned,) * 4 + (whole,) * 4,
        check_vma=False,
    )
```

```python
import jax
import jax.numpy as jnp
from jax import lax
from jax.experimental import pallas as pl
from jax.experimental.pallas import tpu as pltpu
from jax.sharding import Mesh, PartitionSpec as P

BLOCK = 128
W = 128
EPS = 1e-05
BF = jnp.bfloat16
F32 = jnp.float32

SPLIT = {"x": 4, "z": 12, "c": 2, "y": 8}
ALL = ("x", "z", "c", "y")
ROW = ("x", "z", "c")
SCATTER = ("x", "c", "y")
SPREAD = "z"
CHUNK = 1024
WROWS = 1024
UPPER = 4.0
LABEL = 16


def dot(a, b, dims=((1,), (0,))):
    return lax.dot_general(a, b, (dims, ((), ())), preferred_element_type=F32)


TN = ((0,), (0,))
NT = ((1,), (1,))


def full(shape):
    return pl.BlockSpec(shape, memory_space=pltpu.VMEM)


SMEM = pl.BlockSpec(memory_space=pltpu.SMEM)


def row_mean(v):
    return jnp.mean(v, axis=-1, keepdims=True)


def norm_rows(second):
    centred = second - row_mean(second)
    scale = lax.rsqrt(row_mean(centred * centred) + EPS)
    return centred * scale, scale


def norm_back(along, unit, scale):
    return scale * (along - row_mean(along) - unit * row_mean(along * unit))


def silu_parts(first):
    sig = jax.nn.sigmoid(first)
    return (first * sig).astype(BF), sig * (1.0 + first * (1.0 - sig))


def two_halves(v):
    high = v.astype(BF)
    low = (v - high.astype(F32)).astype(BF)
    return high, low


def marks(node, block, shape, dim):
    spot = lax.broadcasted_iota(jnp.int32, shape, dim).astype(F32)
    return jnp.where(node == spot, block, -1.0).astype(BF)


def one_hot(mark, block):
    if not isinstance(block, int):
        block = jnp.full(mark.shape, block.astype(F32)).astype(BF)
    return jnp.where(mark == block, 1.0, 0.0).astype(BF)


def place_of(away):
    return ((away & 1) << 2) | (away & 2) | (away >> 2)


def pack_kernel(blocks, counts, nodes, out):
    n_slots = blocks.shape[0]
    pair = n_slots * BLOCK
    spot = lax.broadcasted_iota(jnp.int32, (LABEL, W), 0)
    for p in range(out.shape[0]):
        label = jnp.zeros((LABEL, W), F32)
        for s in range(n_slots):
            at = pl.multiple_of(blocks[s, p] * BLOCK, BLOCK)
            live = jnp.where(s < counts[0, p], 1.0, 0.0).astype(BF)
            out[p, s * BLOCK : (s + 1) * BLOCK, :] = nodes[pl.ds(at, BLOCK), :] * live
            label = jnp.where(spot == s, blocks[s, p].astype(F32), label)
        out[p, pair:, :] = label.astype(BF)


def early_kernel(nodes, eb, en, feats, ew1, vectors, smark, tmark, joined, partial, cols, *, half):
    rows = feats.shape[0]
    nblk = nodes.shape[0] // BLOCK
    index = jnp.concatenate([eb[...], en[...], eb[...], en[...]], axis=0).astype(F32)
    cols[...] = index.T

    def step(i, carry):
        at = pl.ds(pl.multiple_of(i * CHUNK, CHUNK), CHUNK)
        col = cols[at, :]
        block = col[:, 0:1]
        high = block >= half
        smark[at, :] = marks(col[:, 2:3], jnp.where(high, block - half, block), (CHUNK, BLOCK), 1)
        tm = marks(col[:, 3:4], col[:, 1:2], (CHUNK, BLOCK), 1)
        tmark[at, :] = (tm.astype(F32) + jnp.where(high, UPPER, 0.0)).astype(BF)
        hot_t = jnp.concatenate([one_hot(tm, b) for b in range(nblk)], axis=1)
        joined[at, 0:W] = dot(hot_t, nodes[...]).astype(BF)
        joined[at, W : 2 * W] = feats[at, :]
        partial[at, :] = dot(joined[at, :], ew1[W:, :]) + vectors[0:1, :]
        return carry

    lax.fori_loop(0, rows // CHUNK, step, 0)


def main_kernel(
    lower, upper, incoming, nodes, eb, en, smark, tmark, joined, partial, ecot, ncot,
    ew1, ew2, nw1, nw2, vectors,
    node_new, edge_new, wsum, wide, base,
    ext, gathered, active, unit, slope, scales, summed, dsum, g1, g2,
    *, edge_scale, node_scale,
):
    egain, nb1, ngain = vectors.at[1:2], vectors.at[2:3], vectors.at[3:4]
    rows = joined.shape[0]
    nblk = nodes.shape[0] // BLOCK
    half = ext.shape[0] // BLOCK

    def place(b, block):
        at = (b % half) * BLOCK
        ext[at : at + BLOCK, (b // half) * W : (b // half + 1) * W] = block

    place(0, lower[...])
    for b in range(nblk):
        place(1 + b, nodes[b * BLOCK : (b + 1) * BLOCK, :])
    place(1 + nblk, upper[...])
    n_slots = 2 * (half - 1) // incoming.shape[0]
    for p in range(incoming.shape[0]):
        for k in range(n_slots):
            place(2 + nblk + n_slots * p + k, incoming[p, k * BLOCK : (k + 1) * BLOCK, :])
    summed[...] = jnp.zeros_like(summed)
    g1[...] = jnp.zeros_like(g1)
    g2[...] = jnp.zeros_like(g2)

    def is_upper(at):
        return tmark[at, :].astype(F32) > UPPER - 2.0

    def target_hot(at):
        tm = tmark[at, :].astype(F32)
        tm = jnp.where(tm > UPPER - 2.0, tm - UPPER, tm).astype(BF)
        return jnp.concatenate([one_hot(tm, b) for b in range(nblk)], axis=1)

    def forward(i, carry):
        at = pl.ds(pl.multiple_of(i * CHUNK, CHUNK), CHUNK)
        sm = smark[at, :]
        hot = jnp.concatenate([one_hot(sm, b) for b in range(half)], axis=1)
        both = dot(hot, ext[...])
        source = jnp.where(is_upper(at), both[:, W:], both[:, 0:W]).astype(BF)
        gathered[at, :] = source
        act, slp = silu_parts(partial[at, :] + dot(source, ew1[0:W, :]))
        active[at, :] = act
        slope[at, :] = slp
        u, s = norm_rows(dot(act, ew2[...]))
        unit[at, :] = u
        scales[at, :] = jnp.broadcast_to(s, (CHUNK, W))
        message = (u * egain[...]).astype(BF)
        edge_new[at, :] = (joined[at, W:].astype(F32) + message.astype(F32)).astype(BF)
        row = marks(en[1:2, at].astype(F32), eb[1:2, at].astype(F32), (BLOCK, CHUNK), 0)
        hot_row = jnp.concatenate([one_hot(row, b) for b in range(nblk)], axis=0)
        summed[...] += dot(hot_row, message)
        return carry

    lax.fori_loop(0, rows // CHUNK, forward, 0)

    joined_n = jnp.concatenate([nodes[...], summed[...].astype(BF)], axis=1)
    first = dot(joined_n, nw1[...]) + nb1[...]
    act, slp = silu_parts(first)
    u, s = norm_rows(dot(act, nw2[...]))
    node_new[...] = (nodes[...].astype(F32) + u * ngain[...]).astype(BF)
    upstream = ncot[...].astype(F32)
    d_second = norm_back(upstream * ngain[...], u, s).astype(BF)
    wsum[768:896, :] = (dot(act, d_second, TN) * node_scale).astype(BF)
    d_first = (dot(d_second, nw2[...], NT) * slp).astype(BF)
    wsum[512:768, :] = (dot(joined_n, d_first, TN) * node_scale).astype(BF)
    d_joined = dot(d_first, nw1[...], NT)
    base[...] = upstream + d_joined[:, 0:W]
    high, low = two_halves(d_joined[:, W:])
    dsum[:, 0:W] = high
    dsum[:, W:] = low

    def backward(i, carry):
        at = pl.ds(pl.multiple_of(i * CHUNK, CHUNK), CHUNK)
        both = dot(target_hot(at), dsum[...])
        d_message = both[:, 0:W] + both[:, W:] + ecot[at, :].astype(F32)
        d_second = norm_back(d_message * egain[...], unit[at, :], scales[at, :]).astype(BF)
        g2[...] += dot(d_second, active[at, :], TN)
        d_first = (dot(d_second, ew2[...], NT) * slope[at, :]).astype(BF)
        high = jnp.where(is_upper(at), d_first.astype(F32), 0.0).astype(BF)
        wide[at, 0:W] = d_first - high
        wide[at, W:] = high
        sources = jnp.concatenate([gathered[at, :], joined[at, :]], axis=1)
        g1[...] += dot(d_first, sources, TN)
        return carry

    lax.fori_loop(0, rows // CHUNK, backward, 0)
    wsum[0:384, :] = (g1[...].T * edge_scale).astype(BF)
    wsum[384:512, :] = (g2[...].T * edge_scale).astype(BF)
    wsum[896:, :] = jnp.zeros_like(wsum[896:, :])


def back_kernel(
    me, eb, en, incoming, wide, ecot, ew1,
    far, near, to_lower, to_upper, own, target, edge_grad,
    places, *, half,
):
    rows = wide.shape[0]
    d = wide[:, 0:W] + wide[:, W:]
    nblk = own.shape[0] // BLOCK
    peers, n_slots = incoming.shape[0], incoming.shape[1] // BLOCK
    names = n_slots * BLOCK
    rim_blocks = nblk + 2
    block = eb[0:1, :].astype(F32)
    node = en[...].astype(F32)
    owned = block
    for p in range(peers):
        for s in range(n_slots):
            there = incoming[p, names + s : names + s + 1, 0:1].astype(F32)
            there = there + float(rim_blocks + nblk * p)
            owned = jnp.where(block == float(rim_blocks + n_slots * p + s), there, owned)
    owned = jnp.where(owned >= half, owned - half, owned)
    smark = marks(node[0:1, :], owned, (BLOCK, rows), 0)

    def store(b, sums):
        if b == 0:
            to_lower[...] = sums.astype(BF)
        elif b <= nblk:
            own[(b - 1) * BLOCK : b * BLOCK, :] = sums
        elif b == nblk + 1:
            to_upper[...] = sums.astype(BF)
        else:
            q, j = divmod(b - rim_blocks, nblk)
            places[place_of(q ^ me[0]), j * BLOCK : (j + 1) * BLOCK, :] = sums

    for b in range(0, half, 2):
        sums = dot(jnp.concatenate([one_hot(smark, b), one_hot(smark, b + 1)], axis=0), wide[...])
        for k in range(2):
            store(b + k, sums[k * BLOCK : (k + 1) * BLOCK, 0:W])
            store(b + k + half, sums[k * BLOCK : (k + 1) * BLOCK, W:])
    for place in range(peers):
        if place < peers // 2:
            near[place] = places[place]
        else:
            far[place - peers // 2] = places[place].astype(BF)
    tmark = marks(node[1:2, :], eb[1:2, :].astype(F32), (BLOCK, rows), 0)
    target[...] = dot(jnp.concatenate([one_hot(tmark, b) for b in range(nblk)], axis=0), d)
    edge_grad[...] = (ecot[...].astype(F32) + dot(d, ew1[2 * W :, :], NT)).astype(BF)


def fold_kernel(*refs):
    near, arrived, keep, send = refs[-4:]
    count = keep.shape[0]
    for k in range(2 * count):
        total = near[k] + arrived[k].astype(F32)
        if k < count:
            keep[k] = total
        else:
            send[k - count] = total.astype(BF)


def finish_kernel(near, arrived, from_lower, from_upper, own, target, base, ew1, out, total):
    nblk = own.shape[0] // BLOCK
    total[...] = own[...] + near[0] + arrived[0].astype(F32)
    total[0:BLOCK, :] += from_lower[...].astype(F32)
    total[(nblk - 1) * BLOCK :, :] += from_upper[...].astype(F32)
    source_high, source_low = two_halves(total[...])
    target_high, target_low = two_halves(target[...])
    weights = ew1[...]
    out[...] = (
        base[...]
        + dot(source_high, weights[0:W, :], NT)
        + dot(source_low, weights[0:W, :], NT)
        + dot(target_high, weights[W : 2 * W, :], NT)
        + dot(target_low, weights[W : 2 * W, :], NT)
    )


def unpack_kernel(weights, *outs):
    at = 0
    share = weights.shape[1]
    for out in outs:
        for k in range(out.shape[0] // share):
            out[k * share : (k + 1) * share, :] = weights[at].astype(F32)
            at += 1


def add_kernel(*refs):
    pieces, out = refs[-2:]
    total = jnp.sum(pieces[...].astype(F32), axis=0).astype(BF)
    for k in range(out.shape[0]):
        out[k] = total


def exchange(value, axes):
    return lax.all_to_all(value, axes, split_axis=0, concat_axis=0, tiled=True)


def swap(value, bit):
    return lax.ppermute(value, "y", [(i, i ^ bit) for i in range(lax.axis_size("y"))])


def add(pieces, copies, after):
    return call(
        add_kernel,
        arr((copies,) + pieces.shape[1:], BF),
        in_specs=[pl.BlockSpec(memory_space=pl.ANY)] * len(after) + [VM],
    )(*after, pieces)


def fold(after, near, arrived):
    some = [pl.BlockSpec(memory_space=pl.ANY)] * len(after)
    count, *rest = near.shape
    return call(
        fold_kernel,
        (arr((count // 2, *rest), F32), arr((count // 2, *rest), BF)),
        in_specs=some + [VM, VM],
    )(*after, near, arrived)


def call(kernel, outs, scratch=(), in_specs=None, cost=None, grant=24):
    return pl.pallas_call(
        kernel,
        out_shape=outs,
        in_specs=in_specs,
        out_specs=jax.tree.map(lambda o: pl.BlockSpec(memory_space=pltpu.VMEM), outs),
        scratch_shapes=scratch,
        compiler_params=pltpu.CompilerParams(vmem_limit_bytes=grant << 20),
        cost_estimate=cost,
    )


VM = pl.BlockSpec(memory_space=pltpu.VMEM)


def arr(shape, dtype):
    return jax.ShapeDtypeStruct(shape, dtype)


def local(
    nodes, edge_feats, edge_blocks, edge_nodes, send_blocks, send_counts,
    edge_w1, edge_b1, edge_w2, edge_gain, node_w1, node_b1, node_w2, node_gain,
    node_cot, edge_cot,
):
    own_rows = nodes.shape[0]
    edges = edge_feats.shape[0]
    n_col, slots = send_blocks.shape[1:]
    n_row = lax.axis_size(ROW)
    devices = n_row * n_col
    edge_scale = float(edges * devices) ** (-0.5)
    node_scale = float(own_rows * devices) ** (-0.5)
    blocks = send_blocks[0].T
    up = [(i, i + 1) for i in range(n_row - 1)]
    down = [(i + 1, i) for i in range(n_row - 1)]
    eb = edge_blocks.T
    en = edge_nodes.T

    outgoing = call(
        pack_kernel,
        arr((n_col, slots * BLOCK + LABEL, W), BF),
        in_specs=[SMEM, SMEM, VM],
        grant=60,
        cost=pl.CostEstimate(flops=0, bytes_accessed=600000, transcendentals=0),
    )(blocks, send_counts, nodes)
    incoming = exchange(outgoing, "y")
    lower = lax.ppermute(nodes[own_rows - BLOCK :], ROW, up)
    upper = lax.ppermute(nodes[:BLOCK], ROW, down)

    n_ext = own_rows + 2 * BLOCK + n_col * slots * BLOCK
    vectors = jnp.stack([edge_b1, edge_gain, node_b1, node_gain])
    smark, tmark, joined, partial = call(
        lambda *refs: early_kernel(*refs, half=n_ext // BLOCK // 2),
        (
            arr((edges, W), BF),
            arr((edges, W), BF),
            arr((edges, 2 * W), BF),
            arr((edges, W), F32),
        ),
        scratch=[pltpu.VMEM((edges, 8), F32)],
        in_specs=[VM] * 6,
        cost=pl.CostEstimate(flops=2 * 10**8, bytes_accessed=8000000, transcendentals=0),
    )(nodes, eb, en, edge_feats, edge_w1, vectors)
    node_new, edge_new, wsum, wide, base = call(
        lambda *refs: main_kernel(*refs, edge_scale=edge_scale, node_scale=node_scale),
        (
            arr((own_rows, W), BF),
            arr((edges, W), BF),
            arr((WROWS, W), BF),
            arr((edges, 2 * W), BF),
            arr((own_rows, W), F32),
        ),
        scratch=[
            pltpu.VMEM((n_ext // 2, 2 * W), BF),
            pltpu.VMEM((edges, W), BF),
            pltpu.VMEM((edges, W), BF),
            pltpu.VMEM((edges, W), F32),
            pltpu.VMEM((edges, W), F32),
            pltpu.VMEM((edges, W), F32),
            pltpu.VMEM((own_rows, W), F32),
            pltpu.VMEM((own_rows, 2 * W), BF),
            pltpu.VMEM((W, 3 * W), F32),
            pltpu.VMEM((W, W), F32),
        ],
        in_specs=[VM] * 17,
        cost=pl.CostEstimate(flops=4 * 10**9, bytes_accessed=4000000, transcendentals=200000),
    )(
        lower, upper, incoming, nodes, eb, en, smark, tmark,
        joined, partial, edge_cot, node_cot,
        edge_w1, edge_w2, node_w1, node_w2, vectors,
    )

    members = lax.axis_size(SCATTER)
    share = WROWS // members
    spread = lax.axis_size(SPREAD)
    pieces = exchange(wsum.reshape(members, share, W), SCATTER)

    me = lax.axis_index("y").astype(jnp.int32)[None]
    far, near, to_lower, to_upper, own, target, edge_grad = call(
        lambda *refs: back_kernel(*refs, half=n_ext // BLOCK // 2),
        (
            arr((n_col // 2, own_rows, W), BF),
            arr((n_col // 2, own_rows, W), F32),
            arr((BLOCK, W), BF),
            arr((BLOCK, W), BF),
            arr((own_rows, W), F32),
            arr((own_rows, W), F32),
            arr((edges, W), BF),
        ),
        scratch=[pltpu.VMEM((n_col, own_rows, W), F32)],
        in_specs=[SMEM] + [VM] * 6,
        cost=pl.CostEstimate(flops=10**9, bytes_accessed=2000000, transcendentals=0),
    )(me, eb, en, incoming, wide, edge_cot, edge_w1)
    far = swap(far, 1)
    from_lower = lax.ppermute(to_upper, ROW, up)
    from_upper = lax.ppermute(to_lower, ROW, down)

    part = add(pieces, spread, (far, from_lower, from_upper))
    pieces = exchange(part, SPREAD)
    near, far = fold((part,), near, far)
    far = swap(far, 2)
    part = add(pieces, members, (far,))
    weights = exchange(part, SCATTER)
    near, far = fold((part,), near, far)
    far = swap(far, 4)
    node_grad = call(
        finish_kernel,
        arr((own_rows, W), F32),
        scratch=[pltpu.VMEM((own_rows, W), F32)],
        in_specs=[VM] * 8,
        cost=pl.CostEstimate(flops=10**8, bytes_accessed=1000000, transcendentals=0),
    )(near, far, from_lower, from_upper, own, target, base, edge_w1)
    grads = call(
        unpack_kernel,
        tuple(arr((rows, W), F32) for rows in (3 * W, W, 2 * W, W)),
        in_specs=[VM],
    )(weights)
    return (node_new, edge_new, node_grad, edge_grad) + tuple(grads)


def solution(mesh):
    fine = Mesh(mesh.devices.reshape(tuple(SPLIT.values())), tuple(SPLIT))
    whole = P()
    owned = P(ALL)
    return jax.shard_map(
        local,
        mesh=fine,
        in_specs=(owned,) * 6 + (whole,) * 8 + (owned,) * 2,
        out_specs=(owned,) * 4 + (whole,) * 4,
        check_vma=False,
    )
```

```python
import jax
import jax.numpy as jnp
from jax import lax
from jax.experimental import pallas as pl
from jax.experimental.pallas import tpu as pltpu
from jax.sharding import Mesh, PartitionSpec as P

BLOCK = 128
W = 128
EPS = 1e-05
BF = jnp.bfloat16
F32 = jnp.float32

SPLIT = {"x": 4, "z": 12, "c": 2, "y": 8}
ALL = ("x", "z", "c", "y")
ROW = ("x", "z", "c")
SCATTER = ("x", "c", "y")
SPREAD = "z"
CHUNK = 1024
WROWS = 1024
UPPER = 4.0
LABEL = 16


def dot(a, b, dims=((1,), (0,))):
    return lax.dot_general(a, b, (dims, ((), ())), preferred_element_type=F32)


TN = ((0,), (0,))
NT = ((1,), (1,))


def full(shape):
    return pl.BlockSpec(shape, memory_space=pltpu.VMEM)


SMEM = pl.BlockSpec(memory_space=pltpu.SMEM)


def row_mean(v):
    return jnp.mean(v, axis=-1, keepdims=True)


def norm_rows(second):
    centred = second - row_mean(second)
    scale = lax.rsqrt(row_mean(centred * centred) + EPS)
    return centred * scale, scale


def norm_back(along, unit, scale):
    return scale * (along - row_mean(along) - unit * row_mean(along * unit))


def silu_parts(first):
    sig = jax.nn.sigmoid(first)
    return (first * sig).astype(BF), sig * (1.0 + first * (1.0 - sig))


def two_halves(v):
    high = v.astype(BF)
    low = (v - high.astype(F32)).astype(BF)
    return high, low


def marks(node, block, shape, dim):
    spot = lax.broadcasted_iota(jnp.int32, shape, dim).astype(F32)
    return jnp.where(node == spot, block, -1.0).astype(BF)


def one_hot(mark, block):
    if not isinstance(block, int):
        block = jnp.full(mark.shape, block.astype(F32)).astype(BF)
    return jnp.where(mark == block, 1.0, 0.0).astype(BF)


def place_of(away):
    return ((away & 1) << 2) | (away & 2) | (away >> 2)


def rim_places(me, last):
    first_core = me[1] == 0
    return jnp.where(first_core, last, 0), jnp.where(first_core, 0, last)


def pack_kernel(blocks, counts, nodes, out):
    n_slots = blocks.shape[0]
    pair = n_slots * BLOCK
    spot = lax.broadcasted_iota(jnp.int32, (LABEL, W), 0)
    for p in range(out.shape[0]):
        label = jnp.zeros((LABEL, W), F32)
        for s in range(n_slots):
            at = pl.multiple_of(blocks[s, p] * BLOCK, BLOCK)
            live = jnp.where(s < counts[0, p], 1.0, 0.0).astype(BF)
            out[p, s * BLOCK : (s + 1) * BLOCK, :] = nodes[pl.ds(at, BLOCK), :] * live
            label = jnp.where(spot == s, blocks[s, p].astype(F32), label)
        out[p, pair:, :] = label.astype(BF)


def early_kernel(nodes, eb, en, feats, ew1, vectors, smark, tmark, joined, partial, cols, *, half):
    rows = feats.shape[0]
    nblk = nodes.shape[0] // BLOCK
    index = jnp.concatenate([eb[...], en[...], eb[...], en[...]], axis=0).astype(F32)
    cols[...] = index.T

    def step(i, carry):
        at = pl.ds(pl.multiple_of(i * CHUNK, CHUNK), CHUNK)
        col = cols[at, :]
        block = col[:, 0:1]
        high = block >= half
        smark[at, :] = marks(col[:, 2:3], jnp.where(high, block - half, block), (CHUNK, BLOCK), 1)
        tm = marks(col[:, 3:4], col[:, 1:2], (CHUNK, BLOCK), 1)
        tmark[at, :] = (tm.astype(F32) + jnp.where(high, UPPER, 0.0)).astype(BF)
        hot_t = jnp.concatenate([one_hot(tm, b) for b in range(nblk)], axis=1)
        joined[at, 0:W] = dot(hot_t, nodes[...]).astype(BF)
        joined[at, W : 2 * W] = feats[at, :]
        partial[at, :] = dot(joined[at, :], ew1[W:, :]) + vectors[0:1, :]
        return carry

    lax.fori_loop(0, rows // CHUNK, step, 0)


def main_kernel(
    me, near_rim, far_rim, incoming, nodes, eb, en, smark, tmark, joined, partial, ecot, ncot,
    ew1, ew2, nw1, nw2, vectors,
    node_new, edge_new, wsum, wide, base,
    ext, gathered, active, unit, slope, scales, summed, dsum, g1, g2,
    *, edge_scale, node_scale,
):
    egain, nb1, ngain = vectors.at[1:2], vectors.at[2:3], vectors.at[3:4]
    rows = joined.shape[0]
    nblk = nodes.shape[0] // BLOCK
    half = ext.shape[0] // BLOCK

    def place(b, block):
        at = (b % half) * BLOCK
        ext[at : at + BLOCK, (b // half) * W : (b // half + 1) * W] = block

    near_at, far_at = rim_places(me, nblk + 1)
    ext[pl.ds(pl.multiple_of(near_at * BLOCK, BLOCK), BLOCK), 0:W] = near_rim[...]
    ext[pl.ds(pl.multiple_of(far_at * BLOCK, BLOCK), BLOCK), 0:W] = far_rim[...]
    for b in range(nblk):
        place(1 + b, nodes[b * BLOCK : (b + 1) * BLOCK, :])
    n_slots = 2 * (half - 1) // incoming.shape[0]
    for p in range(incoming.shape[0]):
        for k in range(n_slots):
            place(2 + nblk + n_slots * p + k, incoming[p, k * BLOCK : (k + 1) * BLOCK, :])
    summed[...] = jnp.zeros_like(summed)
    g1[...] = jnp.zeros_like(g1)
    g2[...] = jnp.zeros_like(g2)

    def is_upper(at):
        return tmark[at, :].astype(F32) > UPPER - 2.0

    def target_hot(at):
        tm = tmark[at, :].astype(F32)
        tm = jnp.where(tm > UPPER - 2.0, tm - UPPER, tm).astype(BF)
        return jnp.concatenate([one_hot(tm, b) for b in range(nblk)], axis=1)

    def forward(i, carry):
        at = pl.ds(pl.multiple_of(i * CHUNK, CHUNK), CHUNK)
        sm = smark[at, :]
        hot = jnp.concatenate([one_hot(sm, b) for b in range(half)], axis=1)
        both = dot(hot, ext[...])
        source = jnp.where(is_upper(at), both[:, W:], both[:, 0:W]).astype(BF)
        gathered[at, :] = source
        act, slp = silu_parts(partial[at, :] + dot(source, ew1[0:W, :]))
        active[at, :] = act
        slope[at, :] = slp
        u, s = norm_rows(dot(act, ew2[...]))
        unit[at, :] = u
        scales[at, :] = jnp.broadcast_to(s, (CHUNK, W))
        message = (u * egain[...]).astype(BF)
        edge_new[at, :] = (joined[at, W:].astype(F32) + message.astype(F32)).astype(BF)
        row = marks(en[1:2, at].astype(F32), eb[1:2, at].astype(F32), (BLOCK, CHUNK), 0)
        hot_row = jnp.concatenate([one_hot(row, b) for b in range(nblk)], axis=0)
        summed[...] += dot(hot_row, message)
        return carry

    lax.fori_loop(0, rows // CHUNK, forward, 0)

    joined_n = jnp.concatenate([nodes[...], summed[...].astype(BF)], axis=1)
    first = dot(joined_n, nw1[...]) + nb1[...]
    act, slp = silu_parts(first)
    u, s = norm_rows(dot(act, nw2[...]))
    node_new[...] = (nodes[...].astype(F32) + u * ngain[...]).astype(BF)
    upstream = ncot[...].astype(F32)
    d_second = norm_back(upstream * ngain[...], u, s).astype(BF)
    wsum[768:896, :] = (dot(act, d_second, TN) * node_scale).astype(BF)
    d_first = (dot(d_second, nw2[...], NT) * slp).astype(BF)
    wsum[512:768, :] = (dot(joined_n, d_first, TN) * node_scale).astype(BF)
    d_joined = dot(d_first, nw1[...], NT)
    base[...] = upstream + d_joined[:, 0:W]
    high, low = two_halves(d_joined[:, W:])
    dsum[:, 0:W] = high
    dsum[:, W:] = low

    def backward(i, carry):
        at = pl.ds(pl.multiple_of(i * CHUNK, CHUNK), CHUNK)
        both = dot(target_hot(at), dsum[...])
        d_message = both[:, 0:W] + both[:, W:] + ecot[at, :].astype(F32)
        d_second = norm_back(d_message * egain[...], unit[at, :], scales[at, :]).astype(BF)
        g2[...] += dot(d_second, active[at, :], TN)
        d_first = (dot(d_second, ew2[...], NT) * slope[at, :]).astype(BF)
        high = jnp.where(is_upper(at), d_first.astype(F32), 0.0).astype(BF)
        wide[at, 0:W] = d_first - high
        wide[at, W:] = high
        sources = jnp.concatenate([gathered[at, :], joined[at, :]], axis=1)
        g1[...] += dot(d_first, sources, TN)
        return carry

    lax.fori_loop(0, rows // CHUNK, backward, 0)
    wsum[0:384, :] = (g1[...].T * edge_scale).astype(BF)
    wsum[384:512, :] = (g2[...].T * edge_scale).astype(BF)
    wsum[896:, :] = jnp.zeros_like(wsum[896:, :])


def back_kernel(
    me, eb, en, incoming, wide, ecot, ew1,
    far, near, near_rim, far_rim, own, target, edge_grad,
    places, rims, *, half,
):
    rows = wide.shape[0]
    d = wide[:, 0:W] + wide[:, W:]
    nblk = own.shape[0] // BLOCK
    peers, n_slots = incoming.shape[0], incoming.shape[1] // BLOCK
    names = n_slots * BLOCK
    rim_blocks = nblk + 2
    block = eb[0:1, :].astype(F32)
    node = en[...].astype(F32)
    owned = block
    for p in range(peers):
        for s in range(n_slots):
            there = incoming[p, names + s : names + s + 1, 0:1].astype(F32)
            there = there + float(rim_blocks + nblk * p)
            owned = jnp.where(block == float(rim_blocks + n_slots * p + s), there, owned)
    owned = jnp.where(owned >= half, owned - half, owned)
    smark = marks(node[0:1, :], owned, (BLOCK, rows), 0)

    far_at, near_at = rim_places(me, BLOCK)

    def store(b, sums):
        if b == 0:
            rims[pl.ds(pl.multiple_of(far_at, BLOCK), BLOCK), :] = sums
        elif b <= nblk:
            own[(b - 1) * BLOCK : b * BLOCK, :] = sums
        elif b == nblk + 1:
            rims[pl.ds(pl.multiple_of(near_at, BLOCK), BLOCK), :] = sums
        else:
            q, j = divmod(b - rim_blocks, nblk)
            places[place_of(q ^ me[0]), j * BLOCK : (j + 1) * BLOCK, :] = sums

    for b in range(0, half, 2):
        sums = dot(jnp.concatenate([one_hot(smark, b), one_hot(smark, b + 1)], axis=0), wide[...])
        for k in range(2):
            store(b + k, sums[k * BLOCK : (k + 1) * BLOCK, 0:W])
            store(b + k + half, sums[k * BLOCK : (k + 1) * BLOCK, W:])
    for place in range(peers):
        if place < peers // 2:
            near[place] = places[place]
        else:
            far[place - peers // 2] = places[place].astype(BF)
    near_rim[...] = rims[0:BLOCK, :].astype(BF)
    far_rim[...] = rims[BLOCK:, :].astype(BF)
    tmark = marks(node[1:2, :], eb[1:2, :].astype(F32), (BLOCK, rows), 0)
    target[...] = dot(jnp.concatenate([one_hot(tmark, b) for b in range(nblk)], axis=0), d)
    edge_grad[...] = (ecot[...].astype(F32) + dot(d, ew1[2 * W :, :], NT)).astype(BF)


def fold_kernel(*refs):
    near, arrived, keep, send = refs[-4:]
    count = keep.shape[0]
    for k in range(2 * count):
        total = near[k] + arrived[k].astype(F32)
        if k < count:
            keep[k] = total
        else:
            send[k - count] = total.astype(BF)


def finish_kernel(me, near, arrived, near_rim, far_rim, own, target, base, ew1, out, total):
    nblk = own.shape[0] // BLOCK
    total[...] = own[...] + near[0] + arrived[0].astype(F32)
    for at, rim in zip(rim_places(me, (nblk - 1) * BLOCK), (near_rim, far_rim)):
        total[pl.ds(pl.multiple_of(at, BLOCK), BLOCK), :] += rim[...].astype(F32)
    source_high, source_low = two_halves(total[...])
    target_high, target_low = two_halves(target[...])
    weights = ew1[...]
    out[...] = (
        base[...]
        + dot(source_high, weights[0:W, :], NT)
        + dot(source_low, weights[0:W, :], NT)
        + dot(target_high, weights[W : 2 * W, :], NT)
        + dot(target_low, weights[W : 2 * W, :], NT)
    )


def unpack_kernel(weights, *outs):
    at = 0
    share = weights.shape[1]
    for out in outs:
        for k in range(out.shape[0] // share):
            out[k * share : (k + 1) * share, :] = weights[at].astype(F32)
            at += 1


def add_kernel(*refs):
    pieces, out = refs[-2:]
    total = jnp.sum(pieces[...].astype(F32), axis=0).astype(BF)
    for k in range(out.shape[0]):
        out[k] = total


def exchange(value, axes):
    return lax.all_to_all(value, axes, split_axis=0, concat_axis=0, tiled=True)


def swap(value, bit):
    return lax.ppermute(value, "y", [(i, i ^ bit) for i in range(lax.axis_size("y"))])


def add(pieces, copies, after):
    return call(
        add_kernel,
        arr((copies,) + pieces.shape[1:], BF),
        in_specs=[pl.BlockSpec(memory_space=pl.ANY)] * len(after) + [VM],
    )(*after, pieces)


def fold(after, near, arrived):
    some = [pl.BlockSpec(memory_space=pl.ANY)] * len(after)
    count, *rest = near.shape
    return call(
        fold_kernel,
        (arr((count // 2, *rest), F32), arr((count // 2, *rest), BF)),
        in_specs=some + [VM, VM],
    )(*after, near, arrived)


def call(kernel, outs, scratch=(), in_specs=None, cost=None, grant=24):
    return pl.pallas_call(
        kernel,
        out_shape=outs,
        in_specs=in_specs,
        out_specs=jax.tree.map(lambda o: pl.BlockSpec(memory_space=pltpu.VMEM), outs),
        scratch_shapes=scratch,
        compiler_params=pltpu.CompilerParams(vmem_limit_bytes=grant << 20),
        cost_estimate=cost,
    )


VM = pl.BlockSpec(memory_space=pltpu.VMEM)


def arr(shape, dtype):
    return jax.ShapeDtypeStruct(shape, dtype)


def local(
    nodes, edge_feats, edge_blocks, edge_nodes, send_blocks, send_counts,
    edge_w1, edge_b1, edge_w2, edge_gain, node_w1, node_b1, node_w2, node_gain,
    node_cot, edge_cot,
):
    own_rows = nodes.shape[0]
    edges = edge_feats.shape[0]
    n_col, slots = send_blocks.shape[1:]
    n_row = lax.axis_size(ROW)
    devices = n_row * n_col
    edge_scale = float(edges * devices) ** (-0.5)
    node_scale = float(own_rows * devices) ** (-0.5)
    blocks = send_blocks[0].T
    cores = [(0, 1), (1, 0)]
    chips = [pair for i in range(1, n_row - 1, 2) for pair in ((i, i + 1), (i + 1, i))]
    eb = edge_blocks.T
    en = edge_nodes.T

    outgoing = call(
        pack_kernel,
        arr((n_col, slots * BLOCK + LABEL, W), BF),
        in_specs=[SMEM, SMEM, VM],
        grant=60,
        cost=pl.CostEstimate(flops=0, bytes_accessed=600000, transcendentals=0),
    )(blocks, send_counts, nodes)
    incoming = exchange(outgoing, "y")
    me = jnp.stack([lax.axis_index("y"), lax.axis_index("c")]).astype(jnp.int32)
    first_core = me[1] == 0
    head, tail = nodes[:BLOCK], nodes[own_rows - BLOCK :]
    near_rim = lax.ppermute(jnp.where(first_core, tail, head), "c", cores)
    far_rim = lax.ppermute(jnp.where(first_core, head, tail), ROW, chips)

    n_ext = own_rows + 2 * BLOCK + n_col * slots * BLOCK
    vectors = jnp.stack([edge_b1, edge_gain, node_b1, node_gain])
    smark, tmark, joined, partial = call(
        lambda *refs: early_kernel(*refs, half=n_ext // BLOCK // 2),
        (
            arr((edges, W), BF),
            arr((edges, W), BF),
            arr((edges, 2 * W), BF),
            arr((edges, W), F32),
        ),
        scratch=[pltpu.VMEM((edges, 8), F32)],
        in_specs=[VM] * 6,
        cost=pl.CostEstimate(flops=2 * 10**8, bytes_accessed=8000000, transcendentals=0),
    )(nodes, eb, en, edge_feats, edge_w1, vectors)
    node_new, edge_new, wsum, wide, base = call(
        lambda *refs: main_kernel(*refs, edge_scale=edge_scale, node_scale=node_scale),
        (
            arr((own_rows, W), BF),
            arr((edges, W), BF),
            arr((WROWS, W), BF),
            arr((edges, 2 * W), BF),
            arr((own_rows, W), F32),
        ),
        scratch=[
            pltpu.VMEM((n_ext // 2, 2 * W), BF),
            pltpu.VMEM((edges, W), BF),
            pltpu.VMEM((edges, W), BF),
            pltpu.VMEM((edges, W), F32),
            pltpu.VMEM((edges, W), F32),
            pltpu.VMEM((edges, W), F32),
            pltpu.VMEM((own_rows, W), F32),
            pltpu.VMEM((own_rows, 2 * W), BF),
            pltpu.VMEM((W, 3 * W), F32),
            pltpu.VMEM((W, W), F32),
        ],
        in_specs=[SMEM] + [VM] * 17,
        cost=pl.CostEstimate(flops=4 * 10**9, bytes_accessed=4000000, transcendentals=200000),
    )(
        me, near_rim, far_rim, incoming, nodes, eb, en, smark, tmark,
        joined, partial, edge_cot, node_cot,
        edge_w1, edge_w2, node_w1, node_w2, vectors,
    )

    members = lax.axis_size(SCATTER)
    share = WROWS // members
    spread = lax.axis_size(SPREAD)
    pieces = exchange(wsum.reshape(members, share, W), SCATTER)

    far, near, near_back, far_back, own, target, edge_grad = call(
        lambda *refs: back_kernel(*refs, half=n_ext // BLOCK // 2),
        (
            arr((n_col // 2, own_rows, W), BF),
            arr((n_col // 2, own_rows, W), F32),
            arr((BLOCK, W), BF),
            arr((BLOCK, W), BF),
            arr((own_rows, W), F32),
            arr((own_rows, W), F32),
            arr((edges, W), BF),
        ),
        scratch=[pltpu.VMEM((n_col, own_rows, W), F32), pltpu.VMEM((2 * BLOCK, W), F32)],
        in_specs=[SMEM] + [VM] * 6,
        cost=pl.CostEstimate(flops=10**9, bytes_accessed=2000000, transcendentals=0),
    )(me, eb, en, incoming, wide, edge_cot, edge_w1)
    far = swap(far, 1)
    near_back = lax.ppermute(near_back, "c", cores)
    far_back = lax.ppermute(far_back, ROW, chips)

    part = add(pieces, spread, (far, near_back, far_back))
    pieces = exchange(part, SPREAD)
    near, far = fold((part,), near, far)
    far = swap(far, 2)
    part = add(pieces, members, (far,))
    weights = exchange(part, SCATTER)
    near, far = fold((part,), near, far)
    far = swap(far, 4)
    node_grad = call(
        finish_kernel,
        arr((own_rows, W), F32),
        scratch=[pltpu.VMEM((own_rows, W), F32)],
        in_specs=[SMEM] + [VM] * 8,
        cost=pl.CostEstimate(flops=10**8, bytes_accessed=1000000, transcendentals=0),
    )(me, near, far, near_back, far_back, own, target, base, edge_w1)
    grads = call(
        unpack_kernel,
        tuple(arr((rows, W), F32) for rows in (3 * W, W, 2 * W, W)),
        in_specs=[VM],
    )(weights)
    return (node_new, edge_new, node_grad, edge_grad) + tuple(grads)


def solution(mesh):
    fine = Mesh(mesh.devices.reshape(tuple(SPLIT.values())), tuple(SPLIT))
    whole = P()
    owned = P(ALL)
    return jax.shard_map(
        local,
        mesh=fine,
        in_specs=(owned,) * 6 + (whole,) * 8 + (owned,) * 2,
        out_specs=(owned,) * 4 + (whole,) * 4,
        check_vma=False,
    )
```

```python
import jax
import jax.numpy as jnp
from jax import lax
from jax.experimental import pallas as pl
from jax.experimental.pallas import tpu as pltpu
from jax.sharding import Mesh, PartitionSpec as P

BLOCK = 128
W = 128
EPS = 1e-05
BF = jnp.bfloat16
F32 = jnp.float32

SPLIT = {"x": 4, "z": 12, "c": 2, "y": 8}
ALL = ("x", "z", "c", "y")
ROW = ("x", "z", "c")
SCATTER = ("x", "y")
SPREAD = ("z", "c")
CHUNK = 1024
WROWS = 1024
UPPER = 4.0
LABEL = 16


def dot(a, b, dims=((1,), (0,))):
    return lax.dot_general(a, b, (dims, ((), ())), preferred_element_type=F32)


TN = ((0,), (0,))
NT = ((1,), (1,))


def full(shape):
    return pl.BlockSpec(shape, memory_space=pltpu.VMEM)


SMEM = pl.BlockSpec(memory_space=pltpu.SMEM)


def row_mean(v):
    return jnp.mean(v, axis=-1, keepdims=True)


def norm_rows(second):
    centred = second - row_mean(second)
    scale = lax.rsqrt(row_mean(centred * centred) + EPS)
    return centred * scale, scale


def norm_back(along, unit, scale):
    return scale * (along - row_mean(along) - unit * row_mean(along * unit))


def silu_parts(first):
    sig = jax.nn.sigmoid(first)
    return (first * sig).astype(BF), sig * (1.0 + first * (1.0 - sig))


def two_halves(v):
    high = v.astype(BF)
    low = (v - high.astype(F32)).astype(BF)
    return high, low


def marks(node, block, shape, dim):
    spot = lax.broadcasted_iota(jnp.int32, shape, dim).astype(F32)
    return jnp.where(node == spot, block, -1.0).astype(BF)


def one_hot(mark, block):
    if not isinstance(block, int):
        block = jnp.full(mark.shape, block.astype(F32)).astype(BF)
    return jnp.where(mark == block, 1.0, 0.0).astype(BF)


def place_of(away):
    return ((away & 1) << 2) | ((away & 4) >> 1) | ((away & 2) >> 1)


def pack_kernel(blocks, counts, nodes, out):
    n_slots = blocks.shape[0]
    pair = n_slots * BLOCK
    spot = lax.broadcasted_iota(jnp.int32, (LABEL, W), 0)
    for p in range(out.shape[0]):
        label = jnp.zeros((LABEL, W), F32)
        for s in range(n_slots):
            at = pl.multiple_of(blocks[s, p] * BLOCK, BLOCK)
            live = jnp.where(s < counts[0, p], 1.0, 0.0).astype(BF)
            out[p, s * BLOCK : (s + 1) * BLOCK, :] = nodes[pl.ds(at, BLOCK), :] * live
            label = jnp.where(spot == s, blocks[s, p].astype(F32), label)
        out[p, pair:, :] = label.astype(BF)


def early_kernel(nodes, eb, en, feats, ew1, vectors, smark, tmark, joined, partial, cols, *, half):
    rows = feats.shape[0]
    nblk = nodes.shape[0] // BLOCK
    index = jnp.concatenate([eb[...], en[...], eb[...], en[...]], axis=0).astype(F32)
    cols[...] = index.T

    def step(i, carry):
        at = pl.ds(pl.multiple_of(i * CHUNK, CHUNK), CHUNK)
        col = cols[at, :]
        block = col[:, 0:1]
        high = block >= half
        smark[at, :] = marks(col[:, 2:3], jnp.where(high, block - half, block), (CHUNK, BLOCK), 1)
        tm = marks(col[:, 3:4], col[:, 1:2], (CHUNK, BLOCK), 1)
        tmark[at, :] = (tm.astype(F32) + jnp.where(high, UPPER, 0.0)).astype(BF)
        hot_t = jnp.concatenate([one_hot(tm, b) for b in range(nblk)], axis=1)
        joined[at, 0:W] = dot(hot_t, nodes[...]).astype(BF)
        joined[at, W : 2 * W] = feats[at, :]
        partial[at, :] = dot(joined[at, :], ew1[W:, :]) + vectors[0:1, :]
        return carry

    lax.fori_loop(0, rows // CHUNK, step, 0)


def main_kernel(
    lower, upper, incoming, nodes, eb, en, smark, tmark, joined, partial, ecot, ncot,
    ew1, ew2, nw1, nw2, vectors,
    node_new, edge_new, wsum, wide, base,
    ext, gathered, active, unit, slope, scales, summed, dsum, g1, g2,
    *, edge_scale, node_scale,
):
    egain, nb1, ngain = vectors.at[1:2], vectors.at[2:3], vectors.at[3:4]
    rows = joined.shape[0]
    nblk = nodes.shape[0] // BLOCK
    half = ext.shape[0] // BLOCK

    def place(b, block):
        at = (b % half) * BLOCK
        ext[at : at + BLOCK, (b // half) * W : (b // half + 1) * W] = block

    place(0, lower[...])
    for b in range(nblk):
        place(1 + b, nodes[b * BLOCK : (b + 1) * BLOCK, :])
    place(1 + nblk, upper[...])
    n_slots = 2 * (half - 1) // incoming.shape[0]
    for p in range(incoming.shape[0]):
        for k in range(n_slots):
            place(2 + nblk + n_slots * p + k, incoming[p, k * BLOCK : (k + 1) * BLOCK, :])
    summed[...] = jnp.zeros_like(summed)
    g1[...] = jnp.zeros_like(g1)
    g2[...] = jnp.zeros_like(g2)

    def is_upper(at):
        return tmark[at, :].astype(F32) > UPPER - 2.0

    def target_hot(at):
        tm = tmark[at, :].astype(F32)
        tm = jnp.where(tm > UPPER - 2.0, tm - UPPER, tm).astype(BF)
        return jnp.concatenate([one_hot(tm, b) for b in range(nblk)], axis=1)

    def forward(i, carry):
        at = pl.ds(pl.multiple_of(i * CHUNK, CHUNK), CHUNK)
        sm = smark[at, :]
        hot = jnp.concatenate([one_hot(sm, b) for b in range(half)], axis=1)
        both = dot(hot, ext[...])
        source = jnp.where(is_upper(at), both[:, W:], both[:, 0:W]).astype(BF)
        gathered[at, :] = source
        act, slp = silu_parts(partial[at, :] + dot(source, ew1[0:W, :]))
        active[at, :] = act
        slope[at, :] = slp
        u, s = norm_rows(dot(act, ew2[...]))
        unit[at, :] = u
        scales[at, :] = jnp.broadcast_to(s, (CHUNK, W))
        message = (u * egain[...]).astype(BF)
        edge_new[at, :] = (joined[at, W:].astype(F32) + message.astype(F32)).astype(BF)
        row = marks(en[1:2, at].astype(F32), eb[1:2, at].astype(F32), (BLOCK, CHUNK), 0)
        hot_row = jnp.concatenate([one_hot(row, b) for b in range(nblk)], axis=0)
        summed[...] += dot(hot_row, message)
        return carry

    lax.fori_loop(0, rows // CHUNK, forward, 0)

    joined_n = jnp.concatenate([nodes[...], summed[...].astype(BF)], axis=1)
    first = dot(joined_n, nw1[...]) + nb1[...]
    act, slp = silu_parts(first)
    u, s = norm_rows(dot(act, nw2[...]))
    node_new[...] = (nodes[...].astype(F32) + u * ngain[...]).astype(BF)
    upstream = ncot[...].astype(F32)
    d_second = norm_back(upstream * ngain[...], u, s).astype(BF)
    wsum[768:896, :] = (dot(act, d_second, TN) * node_scale).astype(BF)
    d_first = (dot(d_second, nw2[...], NT) * slp).astype(BF)
    wsum[512:768, :] = (dot(joined_n, d_first, TN) * node_scale).astype(BF)
    d_joined = dot(d_first, nw1[...], NT)
    base[...] = upstream + d_joined[:, 0:W]
    high, low = two_halves(d_joined[:, W:])
    dsum[:, 0:W] = high
    dsum[:, W:] = low

    def backward(i, carry):
        at = pl.ds(pl.multiple_of(i * CHUNK, CHUNK), CHUNK)
        both = dot(target_hot(at), dsum[...])
        d_message = both[:, 0:W] + both[:, W:] + ecot[at, :].astype(F32)
        d_second = norm_back(d_message * egain[...], unit[at, :], scales[at, :]).astype(BF)
        g2[...] += dot(d_second, active[at, :], TN)
        d_first = (dot(d_second, ew2[...], NT) * slope[at, :]).astype(BF)
        high = jnp.where(is_upper(at), d_first.astype(F32), 0.0).astype(BF)
        wide[at, 0:W] = d_first - high
        wide[at, W:] = high
        sources = jnp.concatenate([gathered[at, :], joined[at, :]], axis=1)
        g1[...] += dot(d_first, sources, TN)
        return carry

    lax.fori_loop(0, rows // CHUNK, backward, 0)
    wsum[0:384, :] = (g1[...].T * edge_scale).astype(BF)
    wsum[384:512, :] = (g2[...].T * edge_scale).astype(BF)
    wsum[896:, :] = jnp.zeros_like(wsum[896:, :])


def back_kernel(
    me, eb, en, incoming, wide, ecot, ew1,
    far, near, to_lower, to_upper, own, target, edge_grad,
    places, *, half,
):
    rows = wide.shape[0]
    d = wide[:, 0:W] + wide[:, W:]
    nblk = own.shape[0] // BLOCK
    peers, n_slots = incoming.shape[0], incoming.shape[1] // BLOCK
    names = n_slots * BLOCK
    rim_blocks = nblk + 2
    block = eb[0:1, :].astype(F32)
    node = en[...].astype(F32)
    owned = block
    for p in range(peers):
        for s in range(n_slots):
            there = incoming[p, names + s : names + s + 1, 0:1].astype(F32)
            there = there + float(rim_blocks + nblk * p)
            owned = jnp.where(block == float(rim_blocks + n_slots * p + s), there, owned)
    owned = jnp.where(owned >= half, owned - half, owned)
    smark = marks(node[0:1, :], owned, (BLOCK, rows), 0)

    def store(b, sums):
        if b == 0:
            to_lower[...] = sums.astype(BF)
        elif b <= nblk:
            own[(b - 1) * BLOCK : b * BLOCK, :] = sums
        elif b == nblk + 1:
            to_upper[...] = sums.astype(BF)
        else:
            q, j = divmod(b - rim_blocks, nblk)
            places[place_of(q ^ me[0]), j * BLOCK : (j + 1) * BLOCK, :] = sums

    for b in range(0, half, 2):
        sums = dot(jnp.concatenate([one_hot(smark, b), one_hot(smark, b + 1)], axis=0), wide[...])
        for k in range(2):
            store(b + k, sums[k * BLOCK : (k + 1) * BLOCK, 0:W])
            store(b + k + half, sums[k * BLOCK : (k + 1) * BLOCK, W:])
    for place in range(peers):
        if place < peers // 2:
            near[place] = places[place]
        else:
            far[place - peers // 2] = places[place].astype(BF)
    tmark = marks(node[1:2, :], eb[1:2, :].astype(F32), (BLOCK, rows), 0)
    target[...] = dot(jnp.concatenate([one_hot(tmark, b) for b in range(nblk)], axis=0), d)
    edge_grad[...] = (ecot[...].astype(F32) + dot(d, ew1[2 * W :, :], NT)).astype(BF)


def fold_kernel(*refs):
    near, arrived, keep, send = refs[-4:]
    count = keep.shape[0]
    for k in range(2 * count):
        total = near[k] + arrived[k].astype(F32)
        if k < count:
            keep[k] = total
        else:
            send[k - count] = total.astype(BF)


def finish_kernel(near, arrived, from_lower, from_upper, own, target, base, ew1, out, total):
    nblk = own.shape[0] // BLOCK
    total[...] = own[...] + near[0] + arrived[0].astype(F32)
    total[0:BLOCK, :] += from_lower[...].astype(F32)
    total[(nblk - 1) * BLOCK :, :] += from_upper[...].astype(F32)
    source_high, source_low = two_halves(total[...])
    target_high, target_low = two_halves(target[...])
    weights = ew1[...]
    out[...] = (
        base[...]
        + dot(source_high, weights[0:W, :], NT)
        + dot(source_low, weights[0:W, :], NT)
        + dot(target_high, weights[W : 2 * W, :], NT)
        + dot(target_low, weights[W : 2 * W, :], NT)
    )


def unpack_kernel(weights, *outs):
    at = 0
    share = weights.shape[1]
    for out in outs:
        for k in range(out.shape[0] // share):
            out[k * share : (k + 1) * share, :] = weights[at].astype(F32)
            at += 1


def add_kernel(*refs):
    pieces, out = refs[-2:]
    total = jnp.sum(pieces[...].astype(F32), axis=0).astype(BF)
    for k in range(out.shape[0]):
        out[k] = total


def exchange(value, axes):
    return lax.all_to_all(value, axes, split_axis=0, concat_axis=0, tiled=True)


def swap(value, bit):
    return lax.ppermute(value, "y", [(i, i ^ bit) for i in range(lax.axis_size("y"))])


def add(pieces, copies, after):
    return call(
        add_kernel,
        arr((copies,) + pieces.shape[1:], BF),
        in_specs=[pl.BlockSpec(memory_space=pl.ANY)] * len(after) + [VM],
    )(*after, pieces)


def fold(after, near, arrived):
    some = [pl.BlockSpec(memory_space=pl.ANY)] * len(after)
    count, *rest = near.shape
    return call(
        fold_kernel,
        (arr((count // 2, *rest), F32), arr((count // 2, *rest), BF)),
        in_specs=some + [VM, VM],
    )(*after, near, arrived)


def call(kernel, outs, scratch=(), in_specs=None, cost=None, grant=24):
    return pl.pallas_call(
        kernel,
        out_shape=outs,
        in_specs=in_specs,
        out_specs=jax.tree.map(lambda o: pl.BlockSpec(memory_space=pltpu.VMEM), outs),
        scratch_shapes=scratch,
        compiler_params=pltpu.CompilerParams(vmem_limit_bytes=grant << 20),
        cost_estimate=cost,
    )


VM = pl.BlockSpec(memory_space=pltpu.VMEM)


def arr(shape, dtype):
    return jax.ShapeDtypeStruct(shape, dtype)


def local(
    nodes, edge_feats, edge_blocks, edge_nodes, send_blocks, send_counts,
    edge_w1, edge_b1, edge_w2, edge_gain, node_w1, node_b1, node_w2, node_gain,
    node_cot, edge_cot,
):
    own_rows = nodes.shape[0]
    edges = edge_feats.shape[0]
    n_col, slots = send_blocks.shape[1:]
    n_row = lax.axis_size(ROW)
    devices = n_row * n_col
    edge_scale = float(edges * devices) ** (-0.5)
    node_scale = float(own_rows * devices) ** (-0.5)
    blocks = send_blocks[0].T
    up = [(i, i + 1) for i in range(n_row - 1)]
    down = [(i + 1, i) for i in range(n_row - 1)]
    eb = edge_blocks.T
    en = edge_nodes.T

    outgoing = call(
        pack_kernel,
        arr((n_col, slots * BLOCK + LABEL, W), BF),
        in_specs=[SMEM, SMEM, VM],
        grant=60,
        cost=pl.CostEstimate(flops=0, bytes_accessed=600000, transcendentals=0),
    )(blocks, send_counts, nodes)
    incoming = exchange(outgoing, "y")
    lower = lax.ppermute(nodes[own_rows - BLOCK :], ROW, up)
    upper = lax.ppermute(nodes[:BLOCK], ROW, down)

    n_ext = own_rows + 2 * BLOCK + n_col * slots * BLOCK
    vectors = jnp.stack([edge_b1, edge_gain, node_b1, node_gain])
    smark, tmark, joined, partial = call(
        lambda *refs: early_kernel(*refs, half=n_ext // BLOCK // 2),
        (
            arr((edges, W), BF),
            arr((edges, W), BF),
            arr((edges, 2 * W), BF),
            arr((edges, W), F32),
        ),
        scratch=[pltpu.VMEM((edges, 8), F32)],
        in_specs=[VM] * 6,
        cost=pl.CostEstimate(flops=2 * 10**8, bytes_accessed=8000000, transcendentals=0),
    )(nodes, eb, en, edge_feats, edge_w1, vectors)
    node_new, edge_new, wsum, wide, base = call(
        lambda *refs: main_kernel(*refs, edge_scale=edge_scale, node_scale=node_scale),
        (
            arr((own_rows, W), BF),
            arr((edges, W), BF),
            arr((WROWS, W), BF),
            arr((edges, 2 * W), BF),
            arr((own_rows, W), F32),
        ),
        scratch=[
            pltpu.VMEM((n_ext // 2, 2 * W), BF),
            pltpu.VMEM((edges, W), BF),
            pltpu.VMEM((edges, W), BF),
            pltpu.VMEM((edges, W), F32),
            pltpu.VMEM((edges, W), F32),
            pltpu.VMEM((edges, W), F32),
            pltpu.VMEM((own_rows, W), F32),
            pltpu.VMEM((own_rows, 2 * W), BF),
            pltpu.VMEM((W, 3 * W), F32),
            pltpu.VMEM((W, W), F32),
        ],
        in_specs=[VM] * 17,
        cost=pl.CostEstimate(flops=4 * 10**9, bytes_accessed=4000000, transcendentals=200000),
    )(
        lower, upper, incoming, nodes, eb, en, smark, tmark,
        joined, partial, edge_cot, node_cot,
        edge_w1, edge_w2, node_w1, node_w2, vectors,
    )

    members = lax.axis_size(SCATTER)
    share = WROWS // members
    spread = lax.axis_size(SPREAD)
    pieces = exchange(wsum.reshape(members, share, W), SCATTER)

    me = lax.axis_index("y").astype(jnp.int32)[None]
    far, near, to_lower, to_upper, own, target, edge_grad = call(
        lambda *refs: back_kernel(*refs, half=n_ext // BLOCK // 2),
        (
            arr((n_col // 2, own_rows, W), BF),
            arr((n_col // 2, own_rows, W), F32),
            arr((BLOCK, W), BF),
            arr((BLOCK, W), BF),
            arr((own_rows, W), F32),
            arr((own_rows, W), F32),
            arr((edges, W), BF),
        ),
        scratch=[pltpu.VMEM((n_col, own_rows, W), F32)],
        in_specs=[SMEM] + [VM] * 6,
        cost=pl.CostEstimate(flops=10**9, bytes_accessed=2000000, transcendentals=0),
    )(me, eb, en, incoming, wide, edge_cot, edge_w1)
    far = swap(far, 1)
    from_lower = lax.ppermute(to_upper, ROW, up)
    from_upper = lax.ppermute(to_lower, ROW, down)

    part = add(pieces, spread, (far, from_lower, from_upper))
    pieces = exchange(part, SPREAD)
    near, far = fold((part,), near, far)
    far = swap(far, 4)
    part = add(pieces, members, (far,))
    weights = exchange(part, SCATTER)
    near, far = fold((part,), near, far)
    far = swap(far, 2)
    node_grad = call(
        finish_kernel,
        arr((own_rows, W), F32),
        scratch=[pltpu.VMEM((own_rows, W), F32)],
        in_specs=[VM] * 8,
        cost=pl.CostEstimate(flops=10**8, bytes_accessed=1000000, transcendentals=0),
    )(near, far, from_lower, from_upper, own, target, base, edge_w1)
    grads = call(
        unpack_kernel,
        tuple(arr((rows, W), F32) for rows in (3 * W, W, 2 * W, W)),
        in_specs=[VM],
    )(weights)
    return (node_new, edge_new, node_grad, edge_grad) + tuple(grads)


def solution(mesh):
    fine = Mesh(mesh.devices.reshape(tuple(SPLIT.values())), tuple(SPLIT))
    whole = P()
    owned = P(ALL)
    return jax.shard_map(
        local,
        mesh=fine,
        in_specs=(owned,) * 6 + (whole,) * 8 + (owned,) * 2,
        out_specs=(owned,) * 4 + (whole,) * 4,
        check_vma=False,
    )
```
